1024 devices in a mesh: rep: 4 (over y_hi), fsdp: 256 (over z, y_lo, x, core).
Axes of the slice: x: 8, y: 8 (y_hi: 4, y_lo: 2; y = y_hi * 2 + y_lo), z: 8, core: 2. Of those that a mesh axis runs over, the one named last changes fastest.
Arguments:
- acts: bfloat16 [4, 49152, 8192], P('rep', 'fsdp'), may hold values from -24 to 24
- targets: bfloat16 [4, 49152, 128], P('rep', 'fsdp'), may hold values from -6 to 6
- weight: float32 [4, 8192, 128], P('rep', 'fsdp'), may hold values from -5 to 5
- first_moment: float32 [4, 8192, 128], P('rep', 'fsdp'), may hold values from -0.001953125 to 0.001953125
- second_moment: float32 [4, 8192, 128], P('rep', 'fsdp'), may hold values from 3.7252903e-09 to 5.9604645e-08
- gain: float32 [4, 8192], P('rep', 'fsdp'), may hold values from 0.1 to 1.9
- gain_first: float32 [4, 8192], P('rep', 'fsdp'), may hold values from -0.25 to 0.25
- gain_second: float32 [4, 8192], P('rep', 'fsdp'), may hold values from 6.1035156e-05 to 0.0009765625
- base: float32 [8192, 128], P('fsdp'), may hold values from -5 to 5
- momentum: float32 [8192, 128], P('fsdp'), may hold values from -4 to 4
Outputs:
- new_weight: float32 [4, 8192, 128], P('rep', 'fsdp')
- new_gain: float32 [4, 8192], P('rep', 'fsdp')
- new_base: float32 [8192, 128], P('fsdp')
- new_momentum: float32 [8192, 128], P('fsdp')
The draws below stay inside these ranges and needn't reach their ends.
All inputs are finite; a program needn't handle non-finite values.
Results may differ from the reference program's by a relative error of at most 0.0004.
Values may be sent and summed in bfloat16 or wider, within the bound.
A program may use at most 32 MiB of HBM per device.

```python
import math
import jax
import jax.numpy as jnp
from jax import lax

D = 8192
HEAD = 128
TOK_DEV = 192
TOKENS = 49152
N_REP = 4
N_FSDP = 256


def with_spikes(array, key, source, target, shards_of, factor):
    def block_of(dim):
        return (jnp.arange(array.shape[dim]) // (array.shape[dim] // shards_of)).reshape((-1,) + (1,) * (array.ndim - 1 - dim))

    one_side = jax.random.permutation(key, shards_of)[block_of(target)]
    far = (block_of(target) + shards_of // 2) % shards_of
    return jnp.where((block_of(source) == one_side) | (block_of(source) == far), factor * array, array)


def block_levels(stream_key, dims, pieces, smallest, high):
    def one(position, blocks):
        steps = jax.random.uniform(jax.random.fold_in(jax.random.fold_in(stream_key, 6), position), (blocks,), jnp.float32, smallest / len(pieces), high / len(pieces))
        return jnp.repeat(jnp.exp(steps), dims[position] // blocks).reshape((-1,) + (1,) * (len(dims) - position - 1))

    factor_of = one(*pieces[0])
    for cut in pieces[1:]:
        factor_of = factor_of * one(*cut)
    return factor_of


def gaussian(rng, dims, scale, limit, split=(), held_as=jnp.bfloat16):
    level = block_levels(rng, dims, split, -0.22, 0.18) if split else 1.0
    array = jax.random.normal(rng, dims, jnp.float32) * scale * level
    return jnp.minimum(jnp.maximum(array, -limit), limit).astype(held_as)


def bell_draw_with(stream_key, extent, width, reach, cuts, heavy, held_as=jnp.bfloat16):
    array = width * jax.random.normal(stream_key, extent, jnp.float32)
    if cuts:
        array = array * block_levels(stream_key, extent, cuts, -0.22, 0.18)
    return jnp.clip(with_spikes(array, jax.random.fold_in(stream_key, 3), *heavy), -reach, reach).astype(held_as)


def setup_inputs(seed: int = 0) -> dict:
    arg_keys = jax.random.split(jax.random.key(seed), 11)
    acts = bell_draw_with(arg_keys[0], (N_REP, TOKENS, D), 1.0, 24.0, ((0, 4), (1, 256)), (1, 2, 256, 6.0))
    targets = gaussian(arg_keys[1], (N_REP, TOKENS, HEAD), 1.0, 6.0, ((0, 4), (1, 256)))
    weight = gaussian(arg_keys[2], (N_REP, D, HEAD), 1.0, 5.0, ((0, 4), (1, 256)), jnp.float32)
    first_moment = gaussian(arg_keys[3], (N_REP, D, HEAD), (D ** -1), 0.001953125, ((0, 4), (1, 256)), jnp.float32)
    second_moment = jnp.clip(jnp.exp(math.log(5.960464477539063e-08) - 2.7725887 * jax.random.uniform(arg_keys[4], (N_REP, D, HEAD), jnp.float32) ** block_levels(arg_keys[4], (N_REP, D, HEAD), ((0, 4), (1, 256)), -0.2, 0.2)), 3.725290298461914e-09, 5.960464477539063e-08)
    gain = jnp.clip(1.0 + 0.18 * jax.random.normal(arg_keys[5], (N_REP, D), jnp.float32), 0.1, 1.9)
    gain_first = gaussian(arg_keys[6], (N_REP, D), (HEAD * D ** -1), 0.25, ((0, 4), (1, 256)), jnp.float32)
    gain_second = jnp.clip(jnp.exp(math.log(0.0009765625) - 2.7725887 * jax.random.uniform(arg_keys[7], (N_REP, D), jnp.float32) ** block_levels(arg_keys[7], (N_REP, D), ((0, 4), (1, 256)), -0.2, 0.2)), 6.103515625e-05, 0.0009765625)
    base = gaussian(arg_keys[8], (D, HEAD), 1.0, 5.0, ((0, 256),), jnp.float32)
    momentum = gaussian(arg_keys[9], (D, HEAD), 0.5, 4.0, ((0, 256),), jnp.float32)
    return dict(acts=acts, targets=targets, weight=weight, first_moment=first_moment, second_moment=second_moment, gain=gain, gain_first=gain_first, gain_second=gain_second, base=base, momentum=momentum)


norm_eps = 1e-05
adam_eps = 1e-08
beta_first = 0.9
beta_second = 0.95
bias_first = 1.0 - 0.9 ** 50
bias_second = 1.0 - 0.95 ** 50
inner_rate = 0.1
decay_rate = 0.1
outer_rate = 0.7
nesterov = 0.9
mixing = 0.5

def normalize(block_rows):
    wide_rows = block_rows.astype(jnp.float32)
    factor = lax.rsqrt(lax.optimization_barrier(jnp.mean(wide_rows * wide_rows, axis=-1, keepdims=True)) + norm_eps)
    return (wide_rows * factor).astype(jnp.bfloat16)

def adam_step(param, grad, first, second):
    first = beta_first * first + (1.0 - beta_first) * grad
    second = beta_second * second + (1.0 - beta_second) * grad * grad
    update = first / bias_first / (jnp.sqrt(second / bias_second) + adam_eps)
    return param - inner_rate * (update + decay_rate * param)

def replica_sums(inputs, teacher, low_weight, low_gain):
    root_scale = 1.0 / math.sqrt(D)
    gain_wide = low_gain.astype(jnp.float32)
    input_blocks = inputs.reshape(N_FSDP, TOK_DEV, D)
    teacher_blocks = teacher.reshape(N_FSDP, TOK_DEV, HEAD)

    def accumulate(sums, block_pair):
        grad_sum, gain_sum = sums
        block_rows, block_goal = block_pair
        normed = normalize(block_rows)
        hidden = (normed.astype(jnp.float32) * gain_wide).astype(jnp.bfloat16)
        key_rows = jnp.dot(hidden, low_weight, preferred_element_type=jnp.float32) * root_scale
        residual = (key_rows - block_goal.astype(jnp.float32)).astype(jnp.bfloat16)
        grad_sum = grad_sum + lax.dot_general(normed, residual, (((0,), (0,)), ((), ())), preferred_element_type=jnp.float32)
        back_grad = lax.dot_general(residual, low_weight, (((1,), (1,)), ((), ())), preferred_element_type=jnp.float32) * root_scale
        gain_sum = gain_sum + lax.optimization_barrier(jnp.sum(normed.astype(jnp.float32) * back_grad, axis=0))
        return ((grad_sum, gain_sum), None)
    start_sums = (jnp.zeros((D, HEAD), jnp.float32), jnp.zeros((D,), jnp.float32))
    (grad_sum, gain_sum), _ = lax.scan(accumulate, start_sums, (input_blocks, teacher_blocks))
    return (grad_sum, gain_sum)

def reference(acts, targets, weight, first_moment, second_moment, gain, gain_first, gain_second, base, momentum):
    root_scale = 1.0 / math.sqrt(D)
    inner_list = []
    gain_list = []
    for replica in range(N_REP):
        low_weight = weight[replica].astype(jnp.bfloat16)
        low_gain = gain[replica].astype(jnp.bfloat16)
        grad_sum, gain_sum = replica_sums(acts[replica], targets[replica], low_weight, low_gain)
        grad_weight = low_gain.astype(jnp.float32)[:, None] * grad_sum * root_scale / TOKENS
        grad_gain = gain_sum / TOKENS
        inner_list.append(adam_step(weight[replica], grad_weight, first_moment[replica], second_moment[replica]))
        gain_list.append(adam_step(gain[replica], grad_gain, gain_first[replica], gain_second[replica]))
    inner_weight = jnp.stack(inner_list)
    new_gain = jnp.stack(gain_list)
    sent = base[None] - inner_weight
    average = lax.optimization_barrier(jnp.sum(sent, axis=0)) / N_REP
    new_momentum = nesterov * momentum + average
    new_base = base - outer_rate * (average + nesterov * new_momentum)
    new_weight = mixing * inner_weight + (1.0 - mixing) * new_base[None]
    return (new_weight, new_gain, new_base, new_momentum)
```

```python
import functools
import math

import jax
import jax.numpy as jnp
from jax import lax
from jax.experimental import pallas as pl
from jax.experimental.pallas import tpu as pltpu
from jax.sharding import PartitionSpec as P

MESH = pl.DeviceIdType.MESH

norm_eps = 1e-05
adam_eps = 1e-08
beta_first = 0.9
beta_second = 0.95
bias_first = 1.0 - 0.9**50
bias_second = 1.0 - 0.95**50
inner_rate = 0.1
decay_rate = 0.1
outer_rate = 0.7
nesterov = 0.9
mixing = 0.5

SUBS = 4


def adam_step(param, grad, first, second):
    first = beta_first * first + (1.0 - beta_first) * grad
    second = beta_second * second + (1.0 - beta_second) * grad * grad
    update = first / bias_first / (jnp.sqrt(second / bias_second) + adam_eps)
    return param - inner_rate * (update + decay_rate * param)


def kernel(
    n,
    n_rep,
    acts_hbm,
    targets_hbm,
    weight_hbm,
    first_hbm,
    second_hbm,
    gain_hbm,
    gain_first_hbm,
    gain_second_hbm,
    base_hbm,
    momentum_hbm,
    new_weight_ref,
    new_gain_ref,
    new_base_ref,
    new_momentum_ref,
    acts,
    acts_t,
    targets,
    weight,
    first,
    second,
    gain,
    gain_first,
    gain_second,
    base,
    momentum,
    full_w,
    grads,
    from_core,
    out_plus,
    out_minus,
    in_plus,
    in_minus,
    mine,
    from_small,
    half_sum,
    from_y,
    drifts,
    sem_in,
    sem_small,
    sem_gp,
    sem_gm,
    sem_gc,
    sem_rc,
    sem_rp,
    sem_rm,
    sem_rs,
    sem_y,
    sem_rep,
):
    plus, minus = n // 2, n // 2 - 1
    tokens, d_model = acts.shape
    rows = weight.shape[0]
    token_count = tokens * 4 * n * n
    root_scale = 1.0 / math.sqrt(d_model)

    rep = lax.axis_index("rep")
    f = lax.axis_index("fsdp")
    c = lax.rem(f, 2)
    x = lax.rem(lax.div(f, 2), n)
    y = lax.rem(lax.div(f, 2 * n), 2)
    z = lax.div(f, 4 * n)
    s = x * (1 - c) + z * c
    b = z * (1 - c) + x * c

    def wrap(v):
        return lax.rem(v + n, n)

    def dev(ss, bb, yy):
        xx = ss * (1 - c) + bb * c
        zz = bb * (1 - c) + ss * c
        return ((zz * 2 + yy) * n + xx) * 2 + c

    sibling = f + 1 - 2 * c
    y_mate = dev(s, b, 1 - y)
    up, down = dev(s, wrap(b + 1), y), dev(s, wrap(b - 1), y)

    def remote(src, dst, sems, target):
        return pltpu.make_async_remote_copy(
            src_ref=src,
            dst_ref=dst,
            send_sem=sems[0],
            recv_sem=sems[1],
            device_id={"fsdp": target},
            device_id_type=MESH,
        )

    def pair(sem, *at):
        return sem.at[(0, *at)], sem.at[(1, *at)]

    loads = [
        pltpu.make_async_copy(src, dst, sem_in.at[i])
        for i, (src, dst) in enumerate(
            [
                (weight_hbm.at[0], weight),
                (gain_hbm, gain),
                (acts_hbm.at[0], acts),
                (targets_hbm.at[0], targets),
                (first_hbm.at[0], first),
                (second_hbm.at[0], second),
                (gain_first_hbm, gain_first),
                (gain_second_hbm, gain_second),
                (base_hbm, base),
                (momentum_hbm, momentum),
            ]
        )
    ]
    for load in loads:
        load.start()

    barrier = pltpu.get_barrier_semaphore()
    greeted = [sibling, y_mate, up, down]
    greeted += [dev(wrap(s + k), b, y) for k in range(1, n)]
    for target in greeted:
        pl.semaphore_signal(barrier, inc=1, device_id={"fsdp": target}, device_id_type=MESH)
    for k in range(1, n_rep):
        pl.semaphore_signal(
            barrier, inc=1, device_id={"rep": lax.rem(rep + k, n_rep)}, device_id_type=MESH
        )

    loads[0].wait()
    loads[1].wait()
    row_ids = lax.broadcasted_iota(jnp.int32, (rows, rows), 0)
    lane_ids = lax.broadcasted_iota(jnp.int32, (rows, rows), 1)
    eye = row_ids == lane_ids

    def to_column(row):
        return jnp.sum(jnp.where(eye, jnp.broadcast_to(row, (rows, rows)), 0.0), axis=1, keepdims=True)

    def to_row(column):
        return jnp.sum(jnp.where(eye, jnp.broadcast_to(column, (rows, rows)), 0.0), axis=0, keepdims=True)

    gain_used = to_column(gain[...].astype(jnp.bfloat16).astype(jnp.float32))
    low_weight = weight[...].astype(jnp.bfloat16).astype(jnp.float32)
    full_w[c, b, y, s] = (gain_used * low_weight).astype(jnp.bfloat16)
    pl.semaphore_wait(barrier, len(greeted) + n_rep - 1)

    gather_y = remote(full_w.at[c, b, y, s], full_w.at[c, b, y, s], pair(sem_y, 0), y_mate)
    gather_y.start()
    gather_y.wait_recv()
    gather_small = []
    for k in range(1, n):
        gather_small.append(
            remote(
                full_w.at[c, b, :, s],
                full_w.at[c, b, :, s],
                pair(sem_small, k - 1),
                dev(wrap(s + k), b, y),
            )
        )
        gather_small[-1].start()

    loads[2].wait()
    width = d_model // n

    def prepare(i, total):
        columns = pl.ds(pl.multiple_of(i * width, width), width)
        block = acts[:, columns]
        acts_t[columns, :] = block.T
        wide = block.astype(jnp.float32)
        square = wide * wide
        for j in range(width // 128):
            total = total + square[:, j * 128 : (j + 1) * 128]
        return total

    squares = lax.fori_loop(0, n, prepare, jnp.zeros((tokens, 128), jnp.float32))
    factor = lax.rsqrt(jnp.sum(squares, axis=1, keepdims=True) / d_model + norm_eps)

    for copy in gather_small:
        copy.wait_recv()

    half = n // 2

    def part(ref, j):
        return ref.at[j // 2, pl.ds((j % 2) * half, half)]

    def gather_plus(k, j):
        chunk = part(full_w.at[c, wrap(b - k)], j)
        return remote(chunk, chunk, pair(sem_gp, k, j), up)

    def gather_minus(k, j):
        chunk = part(full_w.at[c, wrap(b + k)], j)
        return remote(chunk, chunk, pair(sem_gm, k, j), down)

    def gather_core(i, owner, at):
        chunk = full_w.at[owner, wrap(at)]
        return remote(chunk, chunk, pair(sem_gc, i), sibling)

    core_offsets = [0] + [-1 - k for k in range(plus)] + [1 + k for k in range(minus)]
    for k in range(plus + 1):
        for j in range(SUBS):
            if k > 0:
                gather_plus(k - 1, j).wait_recv()
            if k < plus:
                gather_plus(k, j).start()
            if 0 < k <= minus:
                gather_minus(k - 1, j).wait_recv()
            if k < minus:
                gather_minus(k, j).start()
        if k == 0:
            gather_core(0, c, b).start()
        else:
            gather_core(k, c, b - k).start()
            if k <= minus:
                gather_core(plus + k, c, b + k).start()
    for i, offset in enumerate(core_offsets):
        gather_core(i, 1 - c, s + offset).wait_recv()

    def forward(i, total):
        columns = pl.ds(pl.multiple_of(i * width, width), width)
        pieces = []
        for yy in range(2):
            for xx in range(n):
                pieces.append(full_w[0, i, yy, xx])
                pieces.append(full_w[1, xx, yy, i])
        return total + jnp.dot(
            acts[:, columns], jnp.concatenate(pieces, axis=0), preferred_element_type=jnp.float32
        )

    keys = lax.fori_loop(0, n, forward, jnp.zeros((tokens, 128), jnp.float32))
    loads[3].wait()
    residual = keys * factor * root_scale - targets[...].astype(jnp.float32)
    scaled = (residual * factor).astype(jnp.bfloat16)

    def backward(i, carry):
        columns = pl.ds(pl.multiple_of(i * width, width), width)
        block = jnp.dot(acts_t[columns, :], scaled, preferred_element_type=jnp.float32)
        block = block.astype(jnp.bfloat16)
        at = 0
        for yy in range(2):
            for xx in range(n):
                grads[0, i, yy, xx] = block[at : at + rows]
                grads[1, xx, yy, i] = block[at + rows : at + 2 * rows]
                at += 2 * rows
        return carry

    lax.fori_loop(0, n, backward, 0)

    order = []
    for k in range(plus):
        order.append(plus - k)
        if k < minus:
            order.append(-(minus - k))
    order.append(0)

    def reduce_core(i, at, offset):
        chunk = wrap(at + offset)
        return remote(grads.at[1 - c, chunk], from_core.at[chunk], pair(sem_rc, i), sibling)

    for i, offset in enumerate(order):
        reduce_core(i, s, offset).start()

    def own(chunk, j):
        at = (j // 2, pl.ds((j % 2) * half, half))
        return grads[(c, chunk, *at)].astype(jnp.float32) + from_core[(chunk, *at)].astype(jnp.float32)

    def reduce_plus(k, j):
        return remote(part(out_plus.at[k], j), part(in_plus.at[k], j), pair(sem_rp, k, j), up)

    def reduce_minus(k, j):
        return remote(part(out_minus.at[k], j), part(in_minus.at[k], j), pair(sem_rm, k, j), down)

    def reduce_core_wait(offset):
        i = order.index(offset)
        chunk = wrap(b + offset)
        remote(grads.at[c, chunk], from_core.at[chunk], pair(sem_rc, i), sibling).wait_recv()

    for k in range(plus):
        reduce_core_wait(plus - k)
        if k < minus:
            reduce_core_wait(-(minus - k))
        for j in range(SUBS):
            at = (j // 2, pl.ds((j % 2) * half, half))
            value = own(wrap(b + plus - k), j)
            if k > 0:
                reduce_plus(k - 1, j).wait_recv()
                value = value + in_plus[(k - 1, *at)].astype(jnp.float32)
            out_plus[(k, *at)] = value.astype(jnp.bfloat16)
            reduce_plus(k, j).start()
            if k < minus:
                value = own(wrap(b - (minus - k)), j)
                if k > 0:
                    reduce_minus(k - 1, j).wait_recv()
                    value = value + in_minus[(k - 1, *at)].astype(jnp.float32)
                out_minus[(k, *at)] = value.astype(jnp.bfloat16)
                reduce_minus(k, j).start()
    reduce_core_wait(0)
    for j in range(SUBS):
        at = (j // 2, pl.ds((j % 2) * half, half))
        value = own(b, j)
        reduce_plus(plus - 1, j).wait_recv()
        value = value + in_plus[(plus - 1, *at)].astype(jnp.float32)
        if minus > 0:
            reduce_minus(minus - 1, j).wait_recv()
            value = value + in_minus[(minus - 1, *at)].astype(jnp.float32)
        mine[at] = value.astype(jnp.bfloat16)

    reduce_small = []
    for k in range(1, n):
        peer = wrap(s + k)
        reduce_small.append(
            remote(mine.at[:, peer], from_small.at[k - 1], pair(sem_rs, k - 1), dev(peer, b, y))
        )
        reduce_small[-1].start()
    for load in loads[4:]:
        load.wait()
    total = mine[:, s].astype(jnp.float32)
    for k in range(1, n):
        reduce_small[k - 1].wait_recv()
        total = total + from_small[k - 1].astype(jnp.float32)
    half_sum[...] = total
    reduce_y = remote(half_sum.at[1 - y], from_y, pair(sem_y, 1), y_mate)
    reduce_y.start()
    reduce_y.wait_recv()
    grad_sum = half_sum[y] + from_y[...]

    grad_weight = gain_used * grad_sum * root_scale / token_count
    inner_weight = adam_step(weight[...], grad_weight, first[...], second[...])
    drifts[rep] = base[...] - inner_weight
    rep_copies = []
    for k in range(1, n_rep):
        rep_copies.append(
            pltpu.make_async_remote_copy(
                src_ref=drifts.at[rep],
                dst_ref=drifts.at[rep],
                send_sem=sem_rep.at[0, k - 1],
                recv_sem=sem_rep.at[1, k - 1],
                device_id={"rep": lax.rem(rep + k, n_rep)},
                device_id_type=MESH,
            )
        )
        rep_copies[-1].start()

    gain_sum = to_row(jnp.sum(grad_sum * low_weight, axis=1, keepdims=True) * root_scale)
    new_gain_ref[...] = adam_step(gain[...], gain_sum / token_count, gain_first[...], gain_second[...])

    for copy in rep_copies:
        copy.wait_recv()
    average = drifts[0]
    for k in range(1, n_rep):
        average = average + drifts[k]
    average = average / n_rep
    new_momentum = nesterov * momentum[...] + average
    new_base = base[...] - outer_rate * (average + nesterov * new_momentum)
    new_momentum_ref[...] = new_momentum
    new_base_ref[...] = new_base
    new_weight_ref[0] = mixing * inner_weight + (1.0 - mixing) * new_base

    gather_y.wait_send()
    reduce_y.wait_send()
    for copy in gather_small + reduce_small + rep_copies:
        copy.wait_send()
    for k in range(plus):
        for j in range(SUBS):
            gather_plus(k, j).wait_send()
            reduce_plus(k, j).wait_send()
    for k in range(minus):
        for j in range(SUBS):
            gather_minus(k, j).wait_send()
            reduce_minus(k, j).wait_send()
    for i, offset in enumerate(core_offsets):
        gather_core(i, c, b + offset).wait_send()
    for i, offset in enumerate(order):
        reduce_core(i, s, offset).wait_send()


def per_device(*args):
    acts, targets, weight, _, _, gain = args[:6]
    n_rep = lax.axis_size("rep")
    n = math.isqrt(lax.axis_size("fsdp") // 4)
    plus, minus = n // 2, max(n // 2 - 1, 1)
    tokens, d_model = acts.shape[1:]
    rows, head = weight.shape[1:]
    low, wide = jnp.bfloat16, jnp.float32
    chunk = (2, n, rows, head)
    dma = pltpu.SemaphoreType.DMA
    scratch = [
        pltpu.VMEM((tokens, d_model), low),
        pltpu.VMEM((d_model, tokens), low),
        pltpu.VMEM((tokens, head), low),
        pltpu.VMEM((rows, head), wide),
        pltpu.VMEM((rows, head), wide),
        pltpu.VMEM((rows, head), wide),
        pltpu.VMEM((1, rows), wide),
        pltpu.VMEM((1, rows), wide),
        pltpu.VMEM((1, rows), wide),
        pltpu.VMEM((rows, head), wide),
        pltpu.VMEM((rows, head), wide),
        pltpu.VMEM((2, n, *chunk), low),
        pltpu.VMEM((2, n, *chunk), low),
        pltpu.VMEM((n, *chunk), low),
        pltpu.VMEM((plus, *chunk), low),
        pltpu.VMEM((minus, *chunk), low),
        pltpu.VMEM((plus, *chunk), low),
        pltpu.VMEM((minus, *chunk), low),
        pltpu.VMEM(chunk, low),
        pltpu.VMEM((n - 1, 2, rows, head), low),
        pltpu.VMEM((2, rows, head), wide),
        pltpu.VMEM((rows, head), wide),
        pltpu.VMEM((n_rep, rows, head), wide),
        dma((10,)),
        dma((2, n - 1)),
        dma((2, plus, SUBS)),
        dma((2, minus, SUBS)),
        dma((2, n)),
        dma((2, n)),
        dma((2, plus, SUBS)),
        dma((2, minus, SUBS)),
        dma((2, n - 1)),
        dma((2, 2)),
        dma((2, max(n_rep - 1, 1))),
    ]
    shape = jax.ShapeDtypeStruct
    return pl.pallas_call(
        functools.partial(kernel, n, n_rep),
        out_shape=(
            shape((1, rows, head), wide),
            shape((1, rows), wide),
            shape((rows, head), wide),
            shape((rows, head), wide),
        ),
        in_specs=[pl.BlockSpec(memory_space=pl.ANY)] * 10,
        out_specs=tuple([pl.BlockSpec(memory_space=pltpu.VMEM)] * 4),
        scratch_shapes=scratch,
        compiler_params=pltpu.CompilerParams(
            collective_id=0, has_side_effects=True, vmem_limit_bytes=48 * 1024 * 1024
        ),
        cost_estimate=pl.CostEstimate(
            flops=4 * tokens * d_model * head, bytes_accessed=2 * tokens * d_model, transcendentals=0
        ),
    )(*args)


def solution(mesh):
    return jax.shard_map(
        per_device,
        mesh=mesh,
        in_specs=(
            P("rep", "fsdp", None),
            P("rep", "fsdp", None),
            P("rep", "fsdp", None),
            P("rep", "fsdp", None),
            P("rep", "fsdp", None),
            P("rep", "fsdp"),
            P("rep", "fsdp"),
            P("rep", "fsdp"),
            P("fsdp", None),
            P("fsdp", None),
        ),
        out_specs=(P("rep", "fsdp", None), P("rep", "fsdp"), P("fsdp", None), P("fsdp", None)),
        check_vma=False,
    )
```

```python
import functools
import math

import jax
import jax.numpy as jnp
from jax import lax
from jax.experimental import pallas as pl
from jax.experimental.pallas import tpu as pltpu
from jax.sharding import PartitionSpec as P

MESH = pl.DeviceIdType.MESH

norm_eps = 1e-05
adam_eps = 1e-08
beta_first = 0.9
beta_second = 0.95
bias_first = 1.0 - 0.9**50
bias_second = 1.0 - 0.95**50
inner_rate = 0.1
decay_rate = 0.1
outer_rate = 0.7
nesterov = 0.9
mixing = 0.5

SUBS = 4


def adam_step(param, grad, first, second):
    first = beta_first * first + (1.0 - beta_first) * grad
    second = beta_second * second + (1.0 - beta_second) * grad * grad
    update = first / bias_first / (jnp.sqrt(second / bias_second) + adam_eps)
    return param - inner_rate * (update + decay_rate * param)


def kernel(
    n,
    n_rep,
    acts_hbm,
    targets_hbm,
    weight_hbm,
    first_hbm,
    second_hbm,
    gain_hbm,
    gain_first_hbm,
    gain_second_hbm,
    base_hbm,
    momentum_hbm,
    new_weight_ref,
    new_gain_ref,
    new_base_ref,
    new_momentum_ref,
    acts,
    acts_t,
    targets,
    weight,
    first,
    second,
    gain,
    gain_first,
    gain_second,
    base,
    momentum,
    full_w,
    grads,
    keys_t,
    from_core,
    out_far,
    out_three,
    out_two,
    out_one,
    in_far,
    in_three,
    in_two,
    in_one,
    mine,
    from_peers,
    drifts,
    sem_in,
    sem_peers,
    sem_big,
    sem_core,
    sem_rep,
):
    tokens, d_model = acts.shape
    rows = weight.shape[0]
    token_count = tokens * 4 * n * n
    root_scale = 1.0 / math.sqrt(d_model)

    rep = lax.axis_index("rep")
    f = lax.axis_index("fsdp")
    c = lax.rem(f, 2)
    x = lax.rem(lax.div(f, 2), n)
    y = lax.rem(lax.div(f, 2 * n), 2)
    z = lax.div(f, 4 * n)
    s = x * (1 - c) + z * c
    b = z * (1 - c) + x * c

    def wrap(v):
        return lax.rem(v + n, n)

    def dev(ss, bb, yy):
        xx = ss * (1 - c) + bb * c
        zz = bb * (1 - c) + ss * c
        return ((zz * 2 + yy) * n + xx) * 2 + c

    sibling = f + 1 - 2 * c
    up, down = dev(s, wrap(b + 1), y), dev(s, wrap(b - 1), y)
    up_two, down_two = dev(s, wrap(b + 2), y), dev(s, wrap(b - 2), y)

    def remote(src, dst, sems, target):
        return pltpu.make_async_remote_copy(
            src_ref=src,
            dst_ref=dst,
            send_sem=sems[0],
            recv_sem=sems[1],
            device_id={"fsdp": target},
            device_id_type=MESH,
        )

    def pair(sem, *at):
        return sem.at[(0, *at)], sem.at[(1, *at)]

    loads = [
        pltpu.make_async_copy(src, dst, sem_in.at[i])
        for i, (src, dst) in enumerate(
            [
                (weight_hbm.at[0], weight),
                (gain_hbm, gain),
                (acts_hbm.at[0], acts),
                (targets_hbm.at[0], targets),
                (first_hbm.at[0], first),
                (second_hbm.at[0], second),
                (gain_first_hbm, gain_first),
                (gain_second_hbm, gain_second),
                (base_hbm, base),
                (momentum_hbm, momentum),
            ]
        )
    ]
    loads[0].start()
    loads[1].start()

    peers = [(k, d) for k in (4, 3, 5, 2, 6, 1, 7, 0) for d in (1, 0) if k or d]
    barrier = pltpu.get_barrier_semaphore()
    greeted = [sibling, up, down, up_two, down_two]
    greeted += [dev(wrap(s + k), b, lax.rem(y + d, 2)) for k, d in peers]
    for target in greeted:
        pl.semaphore_signal(barrier, inc=1, device_id={"fsdp": target}, device_id_type=MESH)
    for k in range(1, n_rep):
        pl.semaphore_signal(
            barrier, inc=1, device_id={"rep": lax.rem(rep + k, n_rep)}, device_id_type=MESH
        )
    for load in loads[2:]:
        load.start()

    loads[0].wait()
    loads[1].wait()
    row_ids = lax.broadcasted_iota(jnp.int32, (rows, rows), 0)
    lane_ids = lax.broadcasted_iota(jnp.int32, (rows, rows), 1)
    eye = row_ids == lane_ids

    def to_column(row):
        return jnp.sum(jnp.where(eye, jnp.broadcast_to(row, (rows, rows)), 0.0), axis=1, keepdims=True)

    def to_row(column):
        return jnp.sum(jnp.where(eye, jnp.broadcast_to(column, (rows, rows)), 0.0), axis=0, keepdims=True)

    gain_used = to_column(gain[...].astype(jnp.bfloat16).astype(jnp.float32))
    low_weight = weight[...].astype(jnp.bfloat16).astype(jnp.float32)
    full_w[c, b, y, s] = (gain_used * low_weight).astype(jnp.bfloat16)
    pl.semaphore_wait(barrier, len(greeted) + n_rep - 1)

    own_rows = full_w.at[c, b, y, s]
    gather_peers = []
    for i, (k, d) in enumerate(peers):
        target = dev(wrap(s + k), b, lax.rem(y + d, 2))
        gather_peers.append(remote(own_rows, own_rows, pair(sem_peers, 0, i), target))
        gather_peers[-1].start()

    loads[2].wait()
    width = d_model // n

    def prepare(i, total):
        columns = pl.ds(pl.multiple_of(i * width, width), width)
        block = acts[:, columns]
        acts_t[i] = block.T.reshape(2, n, 2, rows, tokens)
        wide = block.astype(jnp.float32)
        square = wide * wide
        for j in range(width // 128):
            total = total + square[:, j * 128 : (j + 1) * 128]
        return total

    squares = lax.fori_loop(0, n, prepare, jnp.zeros((tokens, 128), jnp.float32))
    factor = lax.rsqrt(jnp.sum(squares, axis=1, keepdims=True) / d_model + norm_eps)
    keys_t[...] = jnp.zeros_like(keys_t)
    loads[3].wait()

    for i, (k, d) in enumerate(peers):
        landed = full_w.at[c, b, lax.rem(y + d, 2), wrap(s - k)]
        remote(landed, landed, pair(sem_peers, 0, i), sibling).wait_recv()

    half = n // 2

    def at(j):
        return (j // 2, pl.ds((j % 2) * half, half))

    def part(ref, j):
        return ref.at[at(j)]

    def big(phase, kind, src, dst, target, quarters=range(SUBS)):
        return [
            remote(part(src, j), part(dst, j), pair(sem_big, phase, kind, j), target)
            for j in quarters
        ]

    def gathered(offset):
        return full_w.at[c, wrap(b + offset)]

    def gather_core(i, owner, place):
        chunk = full_w.at[owner, wrap(place)]
        return remote(chunk, chunk, pair(sem_core, 0, i), sibling)

    def chunk_acts(owner, place):
        pieces = []
        for yy in range(2):
            for ss in range(n):
                zz = place * (1 - owner) + ss * owner
                xx = ss * (1 - owner) + place * owner
                pieces.append(acts_t[zz, yy, xx, owner])
        return jnp.concatenate(pieces, axis=0)

    deep = 2 * n * rows

    def forward(owner, place):
        place = wrap(place)
        keys_t[...] += lax.dot_general(
            full_w[owner, place].reshape(deep, 128),
            chunk_acts(owner, place),
            (((0,), (0,)), ((), ())),
            preferred_element_type=jnp.float32,
        )

    core_offsets = [0, -2, 2, -1, 1, -3, 3, -4]

    def send_core(i):
        gather_core(i, c, b + core_offsets[i]).start()

    def from_sibling(i):
        gather_core(i, 1 - c, s + core_offsets[i]).wait_recv()
        forward(1 - c, s + core_offsets[i])

    two_up = big(0, 0, gathered(0), gathered(0), up_two)
    two_down = big(0, 1, gathered(0), gathered(0), down_two)
    one_up = big(0, 2, gathered(0), gathered(0), up)
    one_down = big(0, 3, gathered(0), gathered(0), down)
    three_up = big(0, 4, gathered(-2), gathered(-2), up)
    three_down = big(0, 5, gathered(2), gathered(2), down)
    four_up = big(0, 6, gathered(-2), gathered(-2), up_two, range(2))
    four_down = big(0, 6, gathered(2), gathered(2), down_two, range(2, SUBS))
    two_up_in = big(0, 0, gathered(-2), gathered(-2), up_two)
    two_down_in = big(0, 1, gathered(2), gathered(2), down_two)
    one_up_in = big(0, 2, gathered(-1), gathered(-1), up)
    one_down_in = big(0, 3, gathered(1), gathered(1), down)
    three_up_in = big(0, 4, gathered(-3), gathered(-3), up)
    three_down_in = big(0, 5, gathered(3), gathered(3), down)
    four_in = big(0, 6, gathered(-4), gathered(-4), up_two)

    for j in range(SUBS):
        two_up[j].start()
        two_down[j].start()
    for j in range(SUBS):
        one_up[j].start()
        one_down[j].start()
    send_core(0)
    forward(c, b)
    for j in range(SUBS):
        two_up_in[j].wait_recv()
        if j < 2:
            four_up[j].start()
        three_up[j].start()
        two_down_in[j].wait_recv()
        if j >= 2:
            four_down[j - 2].start()
        three_down[j].start()
    send_core(1)
    send_core(2)
    from_sibling(0)
    for j in range(SUBS):
        one_up_in[j].wait_recv()
        one_down_in[j].wait_recv()
    send_core(3)
    send_core(4)
    for i in range(1, 5):
        forward(c, b + core_offsets[i])
    for i in range(1, 5):
        from_sibling(i)
    for j in range(SUBS):
        three_up_in[j].wait_recv()
        three_down_in[j].wait_recv()
    send_core(5)
    send_core(6)
    forward(c, b + core_offsets[5])
    forward(c, b + core_offsets[6])
    for j in range(SUBS):
        four_in[j].wait_recv()
    send_core(7)
    forward(c, b + core_offsets[7])
    for i in range(5, 8):
        from_sibling(i)

    residual = keys_t[...].T * factor * root_scale - targets[...].astype(jnp.float32)
    scaled = (residual * factor).astype(jnp.bfloat16)

    def backward(owner, place):
        place = wrap(place)
        block = jnp.dot(chunk_acts(owner, place), scaled, preferred_element_type=jnp.float32)
        grads[owner, place] = block.astype(jnp.bfloat16).reshape(2, n, rows, 128)

    offsets = [4, -3, 3, -1, 1, -2, 2, 0]

    def reduce_core(i, owner, place):
        chunk = wrap(place)
        return remote(grads.at[owner, chunk], from_core.at[chunk], pair(sem_core, 1, i), sibling)

    def own(offset, j):
        chunk = wrap(b + offset)
        return grads[(c, chunk, *at(j))].astype(jnp.float32) + from_core[
            (chunk, *at(j))
        ].astype(jnp.float32)

    far_down = big(1, 0, out_far, in_far, down_two, range(2))
    far_up = big(1, 0, out_far, in_far, up_two, range(2, SUBS))
    three = [
        big(1, 1, out_three.at[0], in_three.at[0], down),
        big(1, 2, out_three.at[1], in_three.at[1], up),
    ]
    one = [
        big(1, 3, out_one.at[0], in_one.at[0], down),
        big(1, 4, out_one.at[1], in_one.at[1], up),
    ]
    two = [
        big(1, 5, out_two.at[0], in_two.at[0], down_two),
        big(1, 6, out_two.at[1], in_two.at[1], up_two),
    ]
    far = far_down + far_up

    def pass_on(offset):
        i = offsets.index(offset)
        reduce_core(i, c, b + offset).wait_recv()
        side = int(offset > 0)
        for j in range(SUBS):
            value = own(offset, j)
            if abs(offset) == 2:
                three[side][j].wait_recv()
                value = value + in_three[(side, *at(j))].astype(jnp.float32)
                if j // 2 == side:
                    far[j].wait_recv()
                    value = value + in_far[at(j)].astype(jnp.float32)
            low = value.astype(jnp.bfloat16)
            if offset == 4:
                out_far[at(j)] = low
                far[j].start()
            else:
                box, copies = {3: (out_three, three), 2: (out_two, two), 1: (out_one, one)}[abs(offset)]
                box[(side, *at(j))] = low
                copies[side][j].start()

    lag = 2
    for i, offset in enumerate(offsets):
        backward(1 - c, s + offset)
        reduce_core(i, 1 - c, s + offset).start()
        backward(c, b + offset)
        if i >= lag:
            pass_on(offsets[i - lag])
    for offset in offsets[len(offsets) - lag : -1]:
        pass_on(offset)
    reduce_core(len(offsets) - 1, c, b).wait_recv()
    for j in range(SUBS):
        value = own(0, j)
        for box, copies in ((in_one, one), (in_two, two)):
            for side in range(2):
                copies[side][j].wait_recv()
                value = value + box[(side, *at(j))].astype(jnp.float32)
        mine[at(j)] = value.astype(jnp.bfloat16)

    reduce_peers = []
    for i, (k, d) in enumerate(peers):
        ss, yy = wrap(s + k), lax.rem(y + d, 2)
        reduce_peers.append(
            remote(mine.at[yy, ss], from_peers.at[i], pair(sem_peers, 1, i), dev(ss, b, yy))
        )
        reduce_peers[-1].start()
    for load in loads[4:]:
        load.wait()
    grad_sum = mine[y, s].astype(jnp.float32)
    for i, copy in enumerate(reduce_peers):
        copy.wait_recv()
        grad_sum = grad_sum + from_peers[i].astype(jnp.float32)

    grad_weight = gain_used * grad_sum * root_scale / token_count
    inner_weight = adam_step(weight[...], grad_weight, first[...], second[...])
    drifts[rep] = base[...] - inner_weight
    rep_copies = []
    for k in range(1, n_rep):
        rep_copies.append(
            pltpu.make_async_remote_copy(
                src_ref=drifts.at[rep],
                dst_ref=drifts.at[rep],
                send_sem=sem_rep.at[0, k - 1],
                recv_sem=sem_rep.at[1, k - 1],
                device_id={"rep": lax.rem(rep + k, n_rep)},
                device_id_type=MESH,
            )
        )
        rep_copies[-1].start()

    gain_sum = to_row(jnp.sum(grad_sum * low_weight, axis=1, keepdims=True) * root_scale)
    new_gain_ref[...] = adam_step(gain[...], gain_sum / token_count, gain_first[...], gain_second[...])

    for copy in rep_copies:
        copy.wait_recv()
    average = drifts[0]
    for k in range(1, n_rep):
        average = average + drifts[k]
    average = average / n_rep
    new_momentum = nesterov * momentum[...] + average
    new_base = base[...] - outer_rate * (average + nesterov * new_momentum)
    new_momentum_ref[...] = new_momentum
    new_base_ref[...] = new_base
    new_weight_ref[0] = mixing * inner_weight + (1.0 - mixing) * new_base

    for copy in gather_peers + reduce_peers + rep_copies:
        copy.wait_send()
    for copies in (two_up, two_down, one_up, one_down, three_up, three_down, four_up, four_down):
        for copy in copies:
            copy.wait_send()
    for copies in (far, *three, *two, *one):
        for copy in copies:
            copy.wait_send()
    for i, offset in enumerate(core_offsets):
        gather_core(i, c, b + offset).wait_send()
    for i, offset in enumerate(offsets):
        reduce_core(i, 1 - c, s + offset).wait_send()


def per_device(*args):
    acts, targets, weight, _, _, gain = args[:6]
    n_rep = lax.axis_size("rep")
    n = math.isqrt(lax.axis_size("fsdp") // 4)
    tokens, d_model = acts.shape[1:]
    rows, head = weight.shape[1:]
    low, wide = jnp.bfloat16, jnp.float32
    chunk = (2, n, rows, head)
    dma = pltpu.SemaphoreType.DMA
    scratch = [
        pltpu.VMEM((tokens, d_model), low),
        pltpu.VMEM((n, 2, n, 2, rows, tokens), low),
        pltpu.VMEM((tokens, head), low),
        pltpu.VMEM((rows, head), wide),
        pltpu.VMEM((rows, head), wide),
        pltpu.VMEM((rows, head), wide),
        pltpu.VMEM((1, rows), wide),
        pltpu.VMEM((1, rows), wide),
        pltpu.VMEM((1, rows), wide),
        pltpu.VMEM((rows, head), wide),
        pltpu.VMEM((rows, head), wide),
        pltpu.VMEM((2, n, *chunk), low),
        pltpu.VMEM((2, n, *chunk), low),
        pltpu.VMEM((head, tokens), wide),
        pltpu.VMEM((n, *chunk), low),
        pltpu.VMEM(chunk, low),
        pltpu.VMEM((2, *chunk), low),
        pltpu.VMEM((2, *chunk), low),
        pltpu.VMEM((2, *chunk), low),
        pltpu.VMEM(chunk, low),
        pltpu.VMEM((2, *chunk), low),
        pltpu.VMEM((2, *chunk), low),
        pltpu.VMEM((2, *chunk), low),
        pltpu.VMEM(chunk, low),
        pltpu.VMEM((2 * n - 1, rows, head), low),
        pltpu.VMEM((n_rep, rows, head), wide),
        dma((10,)),
        dma((2, 2, 2 * n - 1)),
        dma((2, 2, 7, SUBS)),
        dma((2, 2, n)),
        dma((2, max(n_rep - 1, 1))),
    ]
    shape = jax.ShapeDtypeStruct
    return pl.pallas_call(
        functools.partial(kernel, n, n_rep),
        out_shape=(
            shape((1, rows, head), wide),
            shape((1, rows), wide),
            shape((rows, head), wide),
            shape((rows, head), wide),
        ),
        in_specs=[pl.BlockSpec(memory_space=pltpu.HBM)] * 10,
        out_specs=tuple([pl.BlockSpec(memory_space=pltpu.VMEM)] * 4),
        scratch_shapes=scratch,
        compiler_params=pltpu.CompilerParams(
            collective_id=0, has_side_effects=True, vmem_limit_bytes=48 * 1024 * 1024
        ),
        cost_estimate=pl.CostEstimate(
            flops=4 * tokens * d_model * head, bytes_accessed=2 * tokens * d_model, transcendentals=0
        ),
    )(*args)


def solution(mesh):
    return jax.shard_map(
        per_device,
        mesh=mesh,
        in_specs=(
            P("rep", "fsdp", None),
            P("rep", "fsdp", None),
            P("rep", "fsdp", None),
            P("rep", "fsdp", None),
            P("rep", "fsdp", None),
            P("rep", "fsdp"),
            P("rep", "fsdp"),
            P("rep", "fsdp"),
            P("fsdp", None),
            P("fsdp", None),
        ),
        out_specs=(P("rep", "fsdp", None), P("rep", "fsdp"), P("fsdp", None), P("fsdp", None)),
        check_vma=False,
    )
```

```python
import functools
import math

import jax
import jax.numpy as jnp
from jax import lax
from jax.experimental import pallas as pl
from jax.experimental.pallas import tpu as pltpu
from jax.sharding import PartitionSpec as P

MESH = pl.DeviceIdType.MESH

norm_eps = 1e-05
adam_eps = 1e-08
beta_first = 0.9
beta_second = 0.95
bias_first = 1.0 - 0.9**50
bias_second = 1.0 - 0.95**50
inner_rate = 0.1
decay_rate = 0.1
outer_rate = 0.7
nesterov = 0.9
mixing = 0.5

SUBS = 4
PLACES = [(0, 0), (0, 1), (0, -1), (1, 0), (1, 1), (1, -1), (0, 2), (0, -2)]
PLACES += [(1, 2), (1, -2), (0, 3), (0, -3), (1, 3), (1, -3), (0, 4), (1, 4)]
MIRROR = [PLACES.index((d, k if k == 4 else -k)) for d, k in PLACES]
FAR_UP, FAR_DOWN = (0, 2), (1, 3)


def adam_step(param, grad, first, second):
    first = beta_first * first + (1.0 - beta_first) * grad
    second = beta_second * second + (1.0 - beta_second) * grad * grad
    update = first / bias_first / (jnp.sqrt(second / bias_second) + adam_eps)
    return param - inner_rate * (update + decay_rate * param)


def kernel(
    n,
    n_rep,
    acts_hbm,
    targets_hbm,
    weight_hbm,
    first_hbm,
    second_hbm,
    gain_hbm,
    gain_first_hbm,
    gain_second_hbm,
    base_hbm,
    inner_ref,
    new_gain_ref,
    average_ref,
    acts,
    acts_t,
    targets,
    weight,
    first,
    second,
    gain,
    gain_first,
    gain_second,
    base,
    full_w,
    grads,
    keys_t,
    from_core,
    out_far,
    out_three,
    out_two,
    out_one,
    in_far,
    in_three,
    in_two,
    in_one,
    mine,
    from_peers,
    drifts,
    sem_in,
    sem_peers,
    sem_big,
    sem_core,
    sem_rep,
):
    tokens, d_model = acts.shape
    rows = weight.shape[0]
    token_count = tokens * 4 * n * n
    root_scale = 1.0 / math.sqrt(d_model)

    rep = lax.axis_index("rep")
    f = lax.axis_index("fsdp")
    c = lax.rem(f, 2)
    x = lax.rem(lax.div(f, 2), n)
    y = lax.rem(lax.div(f, 2 * n), 2)
    z = lax.div(f, 4 * n)
    s = x * (1 - c) + z * c
    b = z * (1 - c) + x * c

    def wrap(v):
        return lax.rem(v + n, n)

    def dev(ss, bb, yy):
        xx = ss * (1 - c) + bb * c
        zz = bb * (1 - c) + ss * c
        return ((zz * 2 + yy) * n + xx) * 2 + c

    sibling = f + 1 - 2 * c
    up, down = dev(s, wrap(b + 1), y), dev(s, wrap(b - 1), y)
    up_two, down_two = dev(s, wrap(b + 2), y), dev(s, wrap(b - 2), y)

    def remote(src, dst, sems, target):
        return pltpu.make_async_remote_copy(
            src_ref=src,
            dst_ref=dst,
            send_sem=sems[0],
            recv_sem=sems[1],
            device_id={"fsdp": target},
            device_id_type=MESH,
        )

    def pair(sem, *at):
        return sem.at[(0, *at)], sem.at[(1, *at)]

    loads = [
        pltpu.make_async_copy(src, dst, sem_in.at[i])
        for i, (src, dst) in enumerate(
            [
                (weight_hbm.at[0], weight),
                (gain_hbm, gain),
                (acts_hbm.at[0], acts),
                (targets_hbm.at[0], targets),
                (first_hbm.at[0], first),
                (second_hbm.at[0], second),
                (gain_first_hbm, gain_first),
                (gain_second_hbm, gain_second),
                (base_hbm, base),
            ]
        )
    ]
    loads[0].start()
    loads[1].start()

    def peer(p):
        d, k = PLACES[p]
        return dev(wrap(s + k), b, lax.rem(y + d, 2))

    barrier = pltpu.get_barrier_semaphore()
    greeted = [sibling, up, down, up_two, down_two]
    greeted += [peer(p) for p in range(1, len(PLACES))]
    for target in greeted:
        pl.semaphore_signal(barrier, inc=1, device_id={"fsdp": target}, device_id_type=MESH)
    for k in range(1, n_rep):
        pl.semaphore_signal(
            barrier, inc=1, device_id={"rep": lax.rem(rep + k, n_rep)}, device_id_type=MESH
        )
    for load in loads[2:]:
        load.start()

    loads[0].wait()
    loads[1].wait()
    row_ids = lax.broadcasted_iota(jnp.int32, (rows, rows), 0)
    lane_ids = lax.broadcasted_iota(jnp.int32, (rows, rows), 1)
    eye = row_ids == lane_ids

    def to_column(row):
        return jnp.sum(jnp.where(eye, jnp.broadcast_to(row, (rows, rows)), 0.0), axis=1, keepdims=True)

    def to_row(column):
        return jnp.sum(jnp.where(eye, jnp.broadcast_to(column, (rows, rows)), 0.0), axis=0, keepdims=True)

    gain_used = to_column(gain[...].astype(jnp.bfloat16).astype(jnp.float32))
    low_weight = weight[...].astype(jnp.bfloat16).astype(jnp.float32)
    full_w[c, b, 0] = (gain_used * low_weight).astype(jnp.bfloat16)
    pl.semaphore_wait(barrier, len(greeted) + n_rep - 1)

    gather_peers = [
        remote(
            full_w.at[c, b, 0],
            full_w.at[c, b, MIRROR[p]],
            (sem_peers.at[0, 0, p], sem_peers.at[1, 0, MIRROR[p]]),
            peer(p),
        )
        for p in range(1, len(PLACES))
    ]
    for copy in reversed(gather_peers):
        copy.start()

    loads[2].wait()
    width = d_model // n

    def prepare(i, total):
        columns = pl.ds(pl.multiple_of(i * width, width), width)
        block = acts[:, columns]
        acts_t[i] = block.T.reshape(2, n, 2, rows, tokens)
        wide = block.astype(jnp.float32)
        square = wide * wide
        for j in range(width // 128):
            total = total + square[:, j * 128 : (j + 1) * 128]
        return total

    squares = lax.fori_loop(0, n, prepare, jnp.zeros((tokens, 128), jnp.float32))
    factor = lax.rsqrt(jnp.sum(squares, axis=1, keepdims=True) / d_model + norm_eps)
    keys_t[...] = jnp.zeros_like(keys_t)
    loads[3].wait()

    def at(j):
        return (pl.ds(j * 4, 4),)

    def part(ref, j):
        return ref.at[at(j)]

    def big(phase, kind, src, dst, target, quarters=range(SUBS)):
        return [
            remote(part(src, j), part(dst, j), pair(sem_big, phase, kind, j), target)
            for j in quarters
        ]

    def gathered(offset):
        return full_w.at[c, wrap(b + offset)]

    def gather_core(i, owner, place):
        chunk = full_w.at[owner, wrap(place)]
        return remote(chunk, chunk, pair(sem_core, 0, i), sibling)

    def chunk_acts(owner, small, place):
        pieces = []
        for d, k in PLACES:
            ss = wrap(small + k)
            zz = place * (1 - owner) + ss * owner
            xx = ss * (1 - owner) + place * owner
            pieces.append(acts_t[zz, lax.rem(y + d, 2), xx, owner])
        return jnp.concatenate(pieces, axis=0)

    deep = 2 * n * rows

    def forward(owner, small, place):
        place = wrap(place)
        keys_t[...] += lax.dot_general(
            full_w[owner, place].reshape(deep, 128),
            chunk_acts(owner, small, place),
            (((0,), (0,)), ((), ())),
            preferred_element_type=jnp.float32,
        )

    core_offsets = [0, -2, 2, -1, 1, -3, 3, -4]

    def gather_core_last(j, owner, place):
        quarter = part(full_w.at[owner, wrap(place)], j)
        return remote(quarter, quarter, pair(sem_core, 0, n - 1 + j), sibling)

    def send_core(i):
        gather_core(i, c, b + core_offsets[i]).start()

    def from_sibling(i):
        if i < n - 1:
            gather_core(i, 1 - c, s + core_offsets[i]).wait_recv()
        else:
            for j in range(SUBS):
                gather_core_last(j, 1 - c, s + core_offsets[i]).wait_recv()
        forward(1 - c, b, s + core_offsets[i])

    def forward_own(i):
        forward(c, s, b + core_offsets[i])

    two_up = big(0, 0, gathered(0), gathered(0), up_two)
    two_down = big(0, 1, gathered(0), gathered(0), down_two)
    one_up = big(0, 2, gathered(0), gathered(0), up)
    one_down = big(0, 3, gathered(0), gathered(0), down)
    three_up = big(0, 4, gathered(-2), gathered(-2), up)
    three_down = big(0, 5, gathered(2), gathered(2), down)
    four_up = big(0, 6, gathered(-2), gathered(-2), up_two, FAR_UP)
    four_down = big(0, 6, gathered(2), gathered(2), down_two, FAR_DOWN)
    two_up_in = big(0, 0, gathered(-2), gathered(-2), up_two)
    two_down_in = big(0, 1, gathered(2), gathered(2), down_two)
    one_up_in = big(0, 2, gathered(-1), gathered(-1), up)
    one_down_in = big(0, 3, gathered(1), gathered(1), down)
    three_up_in = big(0, 4, gathered(-3), gathered(-3), up)
    three_down_in = big(0, 5, gathered(3), gathered(3), down)
    four_in = big(0, 6, gathered(-4), gathered(-4), up_two)

    for j in range(SUBS):
        for p in range(max(4 * j, 1), 4 * j + 4):
            landed = full_w.at[c, b, p]
            remote(landed, landed, pair(sem_peers, 0, p), sibling).wait_recv()
        two_up[j].start()
        two_down[j].start()
        one_up[j].start()
        one_down[j].start()
    send_core(0)
    forward_own(0)
    for j in range(SUBS):
        two_up_in[j].wait_recv()
        if j in FAR_UP:
            four_up[FAR_UP.index(j)].start()
        three_up[j].start()
        two_down_in[j].wait_recv()
        if j in FAR_DOWN:
            four_down[FAR_DOWN.index(j)].start()
        three_down[j].start()
    send_core(1)
    send_core(2)
    from_sibling(0)
    for j in range(SUBS):
        one_up_in[j].wait_recv()
        one_down_in[j].wait_recv()
    send_core(3)
    send_core(4)
    for i in range(1, 5):
        forward_own(i)
    for i in range(1, 5):
        from_sibling(i)
    for j in range(SUBS):
        three_up_in[j].wait_recv()
        three_down_in[j].wait_recv()
    send_core(5)
    send_core(6)
    forward_own(5)
    forward_own(6)
    for j in range(SUBS):
        four_in[j].wait_recv()
        gather_core_last(j, c, b - 4).start()
    forward_own(7)
    for i in range(5, 8):
        from_sibling(i)

    residual = keys_t[...].T * factor * root_scale - targets[...].astype(jnp.float32)
    scaled = (residual * factor).astype(jnp.bfloat16)

    def backward(owner, small, place):
        place = wrap(place)
        block = jnp.dot(chunk_acts(owner, small, place), scaled, preferred_element_type=jnp.float32)
        grads[owner, place] = block.astype(jnp.bfloat16).reshape(2 * n, rows, 128)

    offsets = [4, -3, 3, -1, 1, -2, 2, 0]

    def reduce_core(i, owner, place):
        chunk = wrap(place)
        return remote(grads.at[owner, chunk], from_core.at[chunk], pair(sem_core, 1, i), sibling)

    def own(offset, j):
        chunk = wrap(b + offset)
        return grads[(c, chunk, *at(j))].astype(jnp.float32) + from_core[
            (chunk, *at(j))
        ].astype(jnp.float32)

    far_down = big(1, 0, out_far, in_far, down_two, FAR_DOWN)
    far_up = big(1, 0, out_far, in_far, up_two, FAR_UP)
    three = [
        big(1, 1, out_three.at[0], in_three.at[0], down),
        big(1, 2, out_three.at[1], in_three.at[1], up),
    ]
    one = [
        big(1, 3, out_one.at[0], in_one.at[0], down),
        big(1, 4, out_one.at[1], in_one.at[1], up),
    ]
    two = [
        big(1, 5, out_two.at[0], in_two.at[0], down_two),
        big(1, 6, out_two.at[1], in_two.at[1], up_two),
    ]
    far = {**dict(zip(FAR_DOWN, far_down)), **dict(zip(FAR_UP, far_up))}

    def pass_on(offset):
        i = offsets.index(offset)
        reduce_core(i, c, b + offset).wait_recv()
        side = int(offset > 0)
        for j in reversed(range(SUBS)):
            value = own(offset, j)
            if abs(offset) == 2:
                three[side][j].wait_recv()
                value = value + in_three[(side, *at(j))].astype(jnp.float32)
                if j in (FAR_DOWN, FAR_UP)[side]:
                    far[j].wait_recv()
                    value = value + in_far[at(j)].astype(jnp.float32)
            low = value.astype(jnp.bfloat16)
            if offset == 4:
                out_far[at(j)] = low
                far[j].start()
            else:
                box, copies = {3: (out_three, three), 2: (out_two, two), 1: (out_one, one)}[abs(offset)]
                box[(side, *at(j))] = low
                copies[side][j].start()

    lag = 2
    for i, offset in enumerate(offsets):
        backward(1 - c, b, s + offset)
        reduce_core(i, 1 - c, s + offset).start()
        backward(c, s, b + offset)
        if i >= lag:
            pass_on(offsets[i - lag])
    for offset in offsets[len(offsets) - lag : -1]:
        pass_on(offset)
    reduce_core(len(offsets) - 1, c, b).wait_recv()

    reduce_peers = [
        remote(
            mine.at[p],
            from_peers.at[MIRROR[p]],
            (sem_peers.at[0, 1, p], sem_peers.at[1, 1, MIRROR[p]]),
            peer(p),
        )
        for p in range(1, len(PLACES))
    ]
    for j in reversed(range(SUBS)):
        value = own(0, j)
        for box, copies in ((in_one, one), (in_two, two)):
            for side in range(2):
                copies[side][j].wait_recv()
                value = value + box[(side, *at(j))].astype(jnp.float32)
        mine[at(j)] = value.astype(jnp.bfloat16)
        for p in reversed(range(max(4 * j, 1), 4 * j + 4)):
            reduce_peers[p - 1].start()
    for load in loads[4:]:
        load.wait()
    grad_sum = mine[0].astype(jnp.float32)
    for p in range(1, len(PLACES)):
        remote(mine.at[p], from_peers.at[p], pair(sem_peers, 1, p), sibling).wait_recv()
        grad_sum = grad_sum + from_peers[p].astype(jnp.float32)

    grad_weight = gain_used * grad_sum * root_scale / token_count
    inner_weight = adam_step(weight[...], grad_weight, first[...], second[...])
    drifts[rep] = base[...] - inner_weight
    rep_copies = []
    for k in range(1, n_rep):
        rep_copies.append(
            pltpu.make_async_remote_copy(
                src_ref=drifts.at[rep],
                dst_ref=drifts.at[rep],
                send_sem=sem_rep.at[0, k - 1],
                recv_sem=sem_rep.at[1, k - 1],
                device_id={"rep": lax.rem(rep + k, n_rep)},
                device_id_type=MESH,
            )
        )
        rep_copies[-1].start()

    gain_sum = to_row(jnp.sum(grad_sum * low_weight, axis=1, keepdims=True) * root_scale)
    new_gain_ref[...] = adam_step(gain[...], gain_sum / token_count, gain_first[...], gain_second[...])

    for copy in rep_copies:
        copy.wait_recv()
    average = drifts[0]
    for k in range(1, n_rep):
        average = average + drifts[k]
    average_ref[...] = average / n_rep
    inner_ref[...] = inner_weight

    for copy in gather_peers + reduce_peers + rep_copies:
        copy.wait_send()
    for copies in (two_up, two_down, one_up, one_down, three_up, three_down, four_up, four_down):
        for copy in copies:
            copy.wait_send()
    for copies in (far.values(), *three, *two, *one):
        for copy in copies:
            copy.wait_send()
    for i, offset in enumerate(core_offsets[:-1]):
        gather_core(i, c, b + offset).wait_send()
    for j in range(SUBS):
        gather_core_last(j, c, b - 4).wait_send()
    for i, offset in enumerate(offsets):
        reduce_core(i, 1 - c, s + offset).wait_send()


def per_device(*args):
    acts, targets, weight, _, _, gain = args[:6]
    n_rep = lax.axis_size("rep")
    n = math.isqrt(lax.axis_size("fsdp") // 4)
    tokens, d_model = acts.shape[1:]
    rows, head = weight.shape[1:]
    low, wide = jnp.bfloat16, jnp.float32
    chunk = (2 * n, rows, head)
    dma = pltpu.SemaphoreType.DMA
    scratch = [
        pltpu.VMEM((tokens, d_model), low),
        pltpu.VMEM((n, 2, n, 2, rows, tokens), low),
        pltpu.VMEM((tokens, head), low),
        pltpu.VMEM((rows, head), wide),
        pltpu.VMEM((rows, head), wide),
        pltpu.VMEM((rows, head), wide),
        pltpu.VMEM((1, rows), wide),
        pltpu.VMEM((1, rows), wide),
        pltpu.VMEM((1, rows), wide),
        pltpu.VMEM((rows, head), wide),
        pltpu.VMEM((2, n, *chunk), low),
        pltpu.VMEM((2, n, *chunk), low),
        pltpu.VMEM((head, tokens), wide),
        pltpu.VMEM((n, *chunk), low),
        pltpu.VMEM(chunk, low),
        pltpu.VMEM((2, *chunk), low),
        pltpu.VMEM((2, *chunk), low),
        pltpu.VMEM((2, *chunk), low),
        pltpu.VMEM(chunk, low),
        pltpu.VMEM((2, *chunk), low),
        pltpu.VMEM((2, *chunk), low),
        pltpu.VMEM((2, *chunk), low),
        pltpu.VMEM(chunk, low),
        pltpu.VMEM((2 * n, rows, head), low),
        pltpu.VMEM((n_rep, rows, head), wide),
        dma((9,)),
        dma((2, 2, 2 * n)),
        dma((2, 2, 7, SUBS)),
        dma((2, 2, n + SUBS)),
        dma((2, max(n_rep - 1, 1))),
    ]
    shape = jax.ShapeDtypeStruct
    inner_weight, new_gain, average = pl.pallas_call(
        functools.partial(kernel, n, n_rep),
        out_shape=(
            shape((rows, head), wide),
            shape((1, rows), wide),
            shape((rows, head), wide),
        ),
        in_specs=[pl.BlockSpec(memory_space=pltpu.HBM)] * 9,
        out_specs=tuple([pl.BlockSpec(memory_space=pltpu.VMEM)] * 3),
        scratch_shapes=scratch,
        compiler_params=pltpu.CompilerParams(
            collective_id=0, has_side_effects=True, vmem_limit_bytes=64 * 1024 * 1024
        ),
        cost_estimate=pl.CostEstimate(
            flops=4 * tokens * d_model * head, bytes_accessed=2 * tokens * d_model, transcendentals=0
        ),
    )(*args[:-1])
    base, momentum = args[-2:]
    new_momentum = nesterov * momentum + average
    new_base = base - outer_rate * (average + nesterov * new_momentum)
    new_weight = mixing * inner_weight + (1.0 - mixing) * new_base
    return new_weight[None], new_gain, new_base, new_momentum


def solution(mesh):
    return jax.shard_map(
        per_device,
        mesh=mesh,
        in_specs=(
            P("rep", "fsdp", None),
            P("rep", "fsdp", None),
            P("rep", "fsdp", None),
            P("rep", "fsdp", None),
            P("rep", "fsdp", None),
            P("rep", "fsdp"),
            P("rep", "fsdp"),
            P("rep", "fsdp"),
            P("fsdp", None),
            P("fsdp", None),
        ),
        out_specs=(P("rep", "fsdp", None), P("rep", "fsdp"), P("fsdp", None), P("fsdp", None)),
        check_vma=False,
    )
```

```python
import functools
import math

import jax
import jax.numpy as jnp
from jax import lax
from jax.experimental import pallas as pl
from jax.experimental.pallas import tpu as pltpu
from jax.sharding import PartitionSpec as P

MESH = pl.DeviceIdType.MESH

norm_eps = 1e-05
adam_eps = 1e-08
beta_first = 0.9
beta_second = 0.95
bias_first = 1.0 - 0.9**50
bias_second = 1.0 - 0.95**50
inner_rate = 0.1
decay_rate = 0.1
outer_rate = 0.7
nesterov = 0.9
mixing = 0.5

SUBS = 4
PLACES = [(0, 0), (0, 1), (0, -1), (1, 0), (1, 1), (1, -1), (0, 2), (0, -2)]
PLACES += [(1, 2), (1, -2), (0, 3), (0, -3), (1, 3), (1, -3), (0, 4), (1, 4)]
MIRROR = [PLACES.index((d, k if k == 4 else -k)) for d, k in PLACES]
FAR_UP, FAR_DOWN = (0, 2), (1, 3)


def adam_step(param, grad, first, second):
    first = beta_first * first + (1.0 - beta_first) * grad
    second = beta_second * second + (1.0 - beta_second) * grad * grad
    update = first / bias_first / (jnp.sqrt(second / bias_second) + adam_eps)
    return param - inner_rate * (update + decay_rate * param)


def kernel(
    n,
    n_rep,
    acts_hbm,
    targets_hbm,
    weight_hbm,
    first_hbm,
    second_hbm,
    gain_hbm,
    gain_first_hbm,
    gain_second_hbm,
    base_hbm,
    inner_ref,
    new_gain_ref,
    average_ref,
    acts,
    acts_t,
    targets,
    weight,
    first,
    second,
    gain,
    gain_first,
    gain_second,
    base,
    full_w,
    grads,
    keys_t,
    from_core,
    out_far,
    out_three,
    out_two,
    out_one,
    in_far,
    in_three,
    in_two,
    in_one,
    mine,
    from_peers,
    drifts,
    sem_in,
    sem_peers,
    sem_big,
    sem_core,
    sem_rep,
):
    tokens, d_model = acts.shape
    rows = weight.shape[0]
    token_count = tokens * 4 * n * n
    root_scale = 1.0 / math.sqrt(d_model)

    rep = lax.axis_index("rep")
    f = lax.axis_index("fsdp")
    c = lax.rem(f, 2)
    x = lax.rem(lax.div(f, 2), n)
    y = lax.rem(lax.div(f, 2 * n), 2)
    z = lax.div(f, 4 * n)
    s = x * (1 - c) + z * c
    b = z * (1 - c) + x * c

    small_at = {k: lax.rem(s + n + k, n) for k in range(-4, 5)}
    big_at = {k: lax.rem(b + n + k, n) for k in range(-4, 5)}
    y_at = (y, 1 - y)

    def dev(ss, bb, yy):
        xx = ss * (1 - c) + bb * c
        zz = bb * (1 - c) + ss * c
        return ((zz * 2 + yy) * n + xx) * 2 + c

    sibling = f + 1 - 2 * c
    up, down = dev(s, big_at[1], y), dev(s, big_at[-1], y)
    up_two, down_two = dev(s, big_at[2], y), dev(s, big_at[-2], y)

    def remote(src, dst, sems, target):
        return pltpu.make_async_remote_copy(
            src_ref=src,
            dst_ref=dst,
            send_sem=sems[0],
            recv_sem=sems[1],
            device_id={"fsdp": target},
            device_id_type=MESH,
        )

    started = []

    def go(copy):
        copy.start()
        started.append(copy)

    def pair(sem, *at):
        return sem.at[(0, *at)], sem.at[(1, *at)]

    loads = [
        pltpu.make_async_copy(src, dst, sem_in.at[i])
        for i, (src, dst) in enumerate(
            [
                (weight_hbm.at[0], weight),
                (gain_hbm, gain),
                (acts_hbm.at[0], acts),
                (targets_hbm.at[0], targets),
                (first_hbm.at[0], first),
                (second_hbm.at[0], second),
                (gain_first_hbm, gain_first),
                (gain_second_hbm, gain_second),
                (base_hbm, base),
            ]
        )
    ]
    loads[0].start()
    loads[1].start()

    peers = [dev(small_at[k], b, y_at[d]) for d, k in PLACES]

    barrier = pltpu.get_barrier_semaphore()
    greeted = [{"rep": lax.rem(rep + k, n_rep)} for k in range(1, n_rep)]
    nearby = peers[:0:-1] + [up_two, down_two, up, down, sibling]
    greeted += [{"fsdp": target} for target in nearby]
    for target in greeted:
        pl.semaphore_signal(barrier, inc=1, device_id=target, device_id_type=MESH)
    for load in loads[2:]:
        load.start()

    loads[0].wait()
    loads[1].wait()
    row_ids = lax.broadcasted_iota(jnp.int32, (rows, rows), 0)
    lane_ids = lax.broadcasted_iota(jnp.int32, (rows, rows), 1)
    eye = row_ids == lane_ids

    def to_column(row):
        return jnp.sum(jnp.where(eye, jnp.broadcast_to(row, (rows, rows)), 0.0), axis=1, keepdims=True)

    def to_row(column):
        return jnp.sum(jnp.where(eye, jnp.broadcast_to(column, (rows, rows)), 0.0), axis=0, keepdims=True)

    gain_used = to_column(gain[...].astype(jnp.bfloat16).astype(jnp.float32))
    low_weight = weight[...].astype(jnp.bfloat16).astype(jnp.float32)
    full_w[c, b, 0] = (gain_used * low_weight).astype(jnp.bfloat16)
    pl.semaphore_wait(barrier, len(greeted))

    gather_peers = [
        remote(
            full_w.at[c, b, 0],
            full_w.at[c, b, MIRROR[p]],
            (sem_peers.at[0, 0, p], sem_peers.at[1, 0, MIRROR[p]]),
            peers[p],
        )
        for p in range(1, len(PLACES))
    ]
    for copy in reversed(gather_peers):
        go(copy)

    loads[2].wait()
    width = d_model // n

    def prepare(i, total):
        columns = pl.ds(pl.multiple_of(i * width, width), width)
        block = acts[:, columns]
        acts_t[i] = block.T.reshape(2, n, 2, rows, tokens)
        wide = block.astype(jnp.float32)
        square = wide * wide
        for j in range(width // 128):
            total = total + square[:, j * 128 : (j + 1) * 128]
        return total

    squares = lax.fori_loop(0, n, prepare, jnp.zeros((tokens, 128), jnp.float32))
    factor = lax.rsqrt(jnp.sum(squares, axis=1, keepdims=True) / d_model + norm_eps)
    keys_t[...] = jnp.zeros_like(keys_t)
    loads[3].wait()

    def at(j):
        return (pl.ds(j * 4, 4),)

    def part(ref, j):
        return ref.at[at(j)]

    def big(phase, kind, src, dst, target, quarters=range(SUBS)):
        return [
            remote(part(src, j), part(dst, j), pair(sem_big, phase, kind, j), target)
            for j in quarters
        ]

    def gathered(offset):
        return full_w.at[c, big_at[offset]]

    def gather_core(i, owner, place):
        chunk = full_w.at[owner, place]
        return remote(chunk, chunk, pair(sem_core, 0, i), sibling)

    def chunk_acts(owner, small, place):
        pieces = []
        for d, k in PLACES:
            zz = place * (1 - owner) + small[k] * owner
            xx = small[k] * (1 - owner) + place * owner
            pieces.append(acts_t[zz, y_at[d], xx, owner])
        return jnp.concatenate(pieces, axis=0)

    deep = 2 * n * rows

    def forward(owner, small, place):
        keys_t[...] += lax.dot_general(
            full_w[owner, place].reshape(deep, 128),
            chunk_acts(owner, small, place),
            (((0,), (0,)), ((), ())),
            preferred_element_type=jnp.float32,
        )

    core_offsets = [0, -2, 2, -1, 1, -3, 3, -4]

    def gather_core_last(j, owner, place):
        quarter = part(full_w.at[owner, place], j)
        return remote(quarter, quarter, pair(sem_core, 0, n - 1 + j), sibling)

    def send_core(i):
        go(gather_core(i, c, big_at[core_offsets[i]]))

    def from_sibling(i):
        if i < n - 1:
            gather_core(i, 1 - c, small_at[core_offsets[i]]).wait_recv()
        else:
            for j in range(SUBS):
                gather_core_last(j, 1 - c, small_at[core_offsets[i]]).wait_recv()
        forward(1 - c, big_at, small_at[core_offsets[i]])

    def forward_own(i):
        forward(c, small_at, big_at[core_offsets[i]])

    two_up = big(0, 0, gathered(0), gathered(0), up_two)
    two_down = big(0, 1, gathered(0), gathered(0), down_two)
    one_up = big(0, 2, gathered(0), gathered(0), up)
    one_down = big(0, 3, gathered(0), gathered(0), down)
    three_up = big(0, 4, gathered(-2), gathered(-2), up)
    three_down = big(0, 5, gathered(2), gathered(2), down)
    four_up = big(0, 6, gathered(-2), gathered(-2), up_two, FAR_UP)
    four_down = big(0, 6, gathered(2), gathered(2), down_two, FAR_DOWN)
    two_up_in = big(0, 0, gathered(-2), gathered(-2), up_two)
    two_down_in = big(0, 1, gathered(2), gathered(2), down_two)
    one_up_in = big(0, 2, gathered(-1), gathered(-1), up)
    one_down_in = big(0, 3, gathered(1), gathered(1), down)
    three_up_in = big(0, 4, gathered(-3), gathered(-3), up)
    three_down_in = big(0, 5, gathered(3), gathered(3), down)
    four_in = big(0, 6, gathered(-4), gathered(-4), up_two)

    for j in range(SUBS):
        for p in range(max(4 * j, 1), 4 * j + 4):
            landed = full_w.at[c, b, p]
            remote(landed, landed, pair(sem_peers, 0, p), sibling).wait_recv()
        go(two_up[j])
        go(two_down[j])
        go(one_up[j])
        go(one_down[j])
    send_core(0)
    forward_own(0)
    for j in range(SUBS):
        two_up_in[j].wait_recv()
        if j in FAR_UP:
            go(four_up[FAR_UP.index(j)])
        go(three_up[j])
        two_down_in[j].wait_recv()
        if j in FAR_DOWN:
            go(four_down[FAR_DOWN.index(j)])
        go(three_down[j])
    send_core(1)
    send_core(2)
    from_sibling(0)
    for j in range(SUBS):
        one_up_in[j].wait_recv()
        one_down_in[j].wait_recv()
    send_core(3)
    send_core(4)
    for i in range(1, 5):
        forward_own(i)
    for i in range(1, 5):
        from_sibling(i)
    for j in range(SUBS):
        three_up_in[j].wait_recv()
        three_down_in[j].wait_recv()
    send_core(5)
    send_core(6)
    forward_own(5)
    forward_own(6)
    for j in range(SUBS):
        four_in[j].wait_recv()
        go(gather_core_last(j, c, big_at[-4]))
    forward_own(7)
    for i in range(5, 8):
        from_sibling(i)

    residual = keys_t[...].T * factor * root_scale - targets[...].astype(jnp.float32)
    scaled = (residual * factor).astype(jnp.bfloat16)

    def backward(owner, small, place):
        block = jnp.dot(chunk_acts(owner, small, place), scaled, preferred_element_type=jnp.float32)
        grads[owner, place] = block.astype(jnp.bfloat16).reshape(2 * n, rows, 128)

    offsets = [4, -3, 3, -1, 1, -2, 2, 0]

    def reduce_core(i, owner, place):
        return remote(grads.at[owner, place], from_core.at[place], pair(sem_core, 1, i), sibling)

    def own(offset, j):
        chunk = big_at[offset]
        return grads[(c, chunk, *at(j))].astype(jnp.float32) + from_core[
            (chunk, *at(j))
        ].astype(jnp.float32)

    far_down = big(1, 0, out_far, in_far, down_two, FAR_DOWN)
    far_up = big(1, 0, out_far, in_far, up_two, FAR_UP)
    three = [
        big(1, 1, out_three.at[0], in_three.at[0], down),
        big(1, 2, out_three.at[1], in_three.at[1], up),
    ]
    one = [
        big(1, 3, out_one.at[0], in_one.at[0], down),
        big(1, 4, out_one.at[1], in_one.at[1], up),
    ]
    two = [
        big(1, 5, out_two.at[0], in_two.at[0], down_two),
        big(1, 6, out_two.at[1], in_two.at[1], up_two),
    ]
    far = {**dict(zip(FAR_DOWN, far_down)), **dict(zip(FAR_UP, far_up))}

    def pass_on(*group):
        for offset in group:
            reduce_core(offsets.index(offset), c, big_at[offset]).wait_recv()
        for j in reversed(range(SUBS)):
            for offset in group:
                side = int(offset > 0)
                value = own(offset, j)
                if abs(offset) == 2:
                    three[side][j].wait_recv()
                    value = value + in_three[(side, *at(j))].astype(jnp.float32)
                    if j in (FAR_DOWN, FAR_UP)[side]:
                        far[j].wait_recv()
                        value = value + in_far[at(j)].astype(jnp.float32)
                low = value.astype(jnp.bfloat16)
                if offset == 4:
                    out_far[at(j)] = low
                    go(far[j])
                else:
                    box, copies = {3: (out_three, three), 2: (out_two, two), 1: (out_one, one)}[abs(offset)]
                    box[(side, *at(j))] = low
                    go(copies[side][j])

    for i, offset in enumerate(offsets):
        backward(1 - c, big_at, small_at[offset])
        go(reduce_core(i, 1 - c, small_at[offset]))
        backward(c, small_at, big_at[offset])
        if 2 <= i < 7:
            pass_on(offsets[i - 2])
    pass_on(-2, 2)
    reduce_core(len(offsets) - 1, c, b).wait_recv()

    reduce_peers = [
        remote(
            mine.at[p],
            from_peers.at[MIRROR[p]],
            (sem_peers.at[0, 1, p], sem_peers.at[1, 1, MIRROR[p]]),
            peers[p],
        )
        for p in range(1, len(PLACES))
    ]
    for j in reversed(range(SUBS)):
        value = own(0, j)
        for box, copies in ((in_one, one), (in_two, two)):
            for side in range(2):
                copies[side][j].wait_recv()
                value = value + box[(side, *at(j))].astype(jnp.float32)
        mine[at(j)] = value.astype(jnp.bfloat16)
        for p in reversed(range(max(4 * j, 1), 4 * j + 4)):
            go(reduce_peers[p - 1])
    for load in loads[4:]:
        load.wait()
    grad_sum = mine[0].astype(jnp.float32)
    for p in range(1, len(PLACES)):
        remote(mine.at[p], from_peers.at[p], pair(sem_peers, 1, p), sibling).wait_recv()
        grad_sum = grad_sum + from_peers[p].astype(jnp.float32)

    grad_weight = gain_used * grad_sum * root_scale / token_count
    inner_weight = adam_step(weight[...], grad_weight, first[...], second[...])
    drifts[rep] = base[...] - inner_weight
    rep_copies = []
    for k in range(1, n_rep):
        rep_copies.append(
            pltpu.make_async_remote_copy(
                src_ref=drifts.at[rep],
                dst_ref=drifts.at[rep],
                send_sem=sem_rep.at[0, k - 1],
                recv_sem=sem_rep.at[1, k - 1],
                device_id={"rep": lax.rem(rep + k, n_rep)},
                device_id_type=MESH,
            )
        )
        go(rep_copies[-1])

    gain_sum = to_row(jnp.sum(grad_sum * low_weight, axis=1, keepdims=True) * root_scale)
    new_gain_ref[...] = adam_step(gain[...], gain_sum / token_count, gain_first[...], gain_second[...])

    for copy in rep_copies:
        copy.wait_recv()
    average = drifts[0]
    for k in range(1, n_rep):
        average = average + drifts[k]
    average_ref[...] = average / n_rep
    inner_ref[...] = inner_weight

    for copy in started:
        copy.wait_send()


def per_device(*args):
    acts, targets, weight, _, _, gain = args[:6]
    n_rep = lax.axis_size("rep")
    n = math.isqrt(lax.axis_size("fsdp") // 4)
    tokens, d_model = acts.shape[1:]
    rows, head = weight.shape[1:]
    low, wide = jnp.bfloat16, jnp.float32
    chunk = (2 * n, rows, head)
    dma = pltpu.SemaphoreType.DMA
    scratch = [
        pltpu.VMEM((tokens, d_model), low),
        pltpu.VMEM((n, 2, n, 2, rows, tokens), low),
        pltpu.VMEM((tokens, head), low),
        pltpu.VMEM((rows, head), wide),
        pltpu.VMEM((rows, head), wide),
        pltpu.VMEM((rows, head), wide),
        pltpu.VMEM((1, rows), wide),
        pltpu.VMEM((1, rows), wide),
        pltpu.VMEM((1, rows), wide),
        pltpu.VMEM((rows, head), wide),
        pltpu.VMEM((2, n, *chunk), low),
        pltpu.VMEM((2, n, *chunk), low),
        pltpu.VMEM((head, tokens), wide),
        pltpu.VMEM((n, *chunk), low),
        pltpu.VMEM(chunk, low),
        pltpu.VMEM((2, *chunk), low),
        pltpu.VMEM((2, *chunk), low),
        pltpu.VMEM((2, *chunk), low),
        pltpu.VMEM(chunk, low),
        pltpu.VMEM((2, *chunk), low),
        pltpu.VMEM((2, *chunk), low),
        pltpu.VMEM((2, *chunk), low),
        pltpu.VMEM(chunk, low),
        pltpu.VMEM((2 * n, rows, head), low),
        pltpu.VMEM((n_rep, rows, head), wide),
        dma((9,)),
        dma((2, 2, 2 * n)),
        dma((2, 2, 7, SUBS)),
        dma((2, 2, n + SUBS)),
        dma((2, max(n_rep - 1, 1))),
    ]
    inner_weight, new_gain, average = pl.pallas_call(
        functools.partial(kernel, n, n_rep),
        out_shape=(
            pltpu.VMEM((rows, head), wide),
            pltpu.VMEM((1, rows), wide),
            pltpu.VMEM((rows, head), wide),
        ),
        in_specs=[pl.BlockSpec(memory_space=pltpu.HBM)] * 9,
        out_specs=tuple([pl.BlockSpec(memory_space=pltpu.VMEM)] * 3),
        scratch_shapes=scratch,
        compiler_params=pltpu.CompilerParams(
            collective_id=0, has_side_effects=True, vmem_limit_bytes=48 * 1024 * 1024
        ),
        cost_estimate=pl.CostEstimate(
            flops=4 * tokens * d_model * head, bytes_accessed=2 * tokens * d_model, transcendentals=0
        ),
    )(*[pltpu.with_memory_space_constraint(arg, pltpu.HBM) for arg in args[:-1]])
    base, momentum = args[-2:]
    new_momentum = nesterov * momentum + average
    new_base = base - outer_rate * (average + nesterov * new_momentum)
    new_weight = mixing * inner_weight + (1.0 - mixing) * new_base
    return new_weight[None], new_gain, new_base, new_momentum


def solution(mesh):
    return jax.shard_map(
        per_device,
        mesh=mesh,
        in_specs=(
            P("rep", "fsdp", None),
            P("rep", "fsdp", None),
            P("rep", "fsdp", None),
            P("rep", "fsdp", None),
            P("rep", "fsdp", None),
            P("rep", "fsdp"),
            P("rep", "fsdp"),
            P("rep", "fsdp"),
            P("fsdp", None),
            P("fsdp", None),
        ),
        out_specs=(P("rep", "fsdp", None), P("rep", "fsdp"), P("fsdp", None), P("fsdp", None)),
        check_vma=False,
    )
```

```python
import functools
import math

import jax
import jax.numpy as jnp
from jax import lax
from jax.experimental import pallas as pl
from jax.experimental.pallas import tpu as pltpu
from jax.sharding import PartitionSpec as P

MESH = pl.DeviceIdType.MESH

norm_eps = 1e-05
adam_eps = 1e-08
beta_first = 0.9
beta_second = 0.95
bias_first = 1.0 - 0.9**50
bias_second = 1.0 - 0.95**50
inner_rate = 0.1
decay_rate = 0.1
outer_rate = 0.7
nesterov = 0.9
mixing = 0.5

SUBS = 4
PLACES = [(0, 0), (0, 1), (0, -1), (1, 0), (1, 1), (1, -1), (0, 2), (0, -2)]
PLACES += [(1, 2), (1, -2), (0, 3), (0, -3), (1, 3), (1, -3), (0, 4), (1, 4)]
MIRROR = [PLACES.index((d, k if k == 4 else -k)) for d, k in PLACES]
FAR_UP, FAR_DOWN = (0, 2), (1, 3)


def adam_step(param, grad, first, second):
    first = beta_first * first + (1.0 - beta_first) * grad
    second = beta_second * second + (1.0 - beta_second) * grad * grad
    update = first / bias_first / (jnp.sqrt(second / bias_second) + adam_eps)
    return param - inner_rate * (update + decay_rate * param)


def kernel(
    n,
    n_rep,
    acts_hbm,
    targets_hbm,
    weight_hbm,
    first_hbm,
    second_hbm,
    gain_hbm,
    gain_first_hbm,
    gain_second_hbm,
    base_hbm,
    inner_ref,
    new_gain_ref,
    average_ref,
    acts,
    acts_t,
    targets,
    weight,
    first,
    second,
    gain,
    gain_first,
    gain_second,
    base,
    full_w,
    grads,
    keys_t,
    from_core,
    out_far,
    out_three,
    out_two,
    out_one,
    in_far,
    in_three,
    in_two,
    in_one,
    mine,
    from_peers,
    drifts,
    sem_in,
    sem_send,
    sem_peers,
    sem_big,
    sem_core,
    sem_rep,
):
    tokens, d_model = acts.shape
    rows = weight.shape[0]
    token_count = tokens * 4 * n * n
    root_scale = 1.0 / math.sqrt(d_model)

    rep = lax.axis_index("rep")
    f = lax.axis_index("fsdp")
    c = lax.rem(f, 2)
    x = lax.rem(lax.div(f, 2), n)
    y = lax.rem(lax.div(f, 2 * n), 2)
    z = lax.div(f, 4 * n)
    s = x * (1 - c) + z * c
    b = z * (1 - c) + x * c

    small_at = {k: lax.rem(s + n + k, n) for k in range(-4, 5)}
    big_at = {k: lax.rem(b + n + k, n) for k in range(-4, 5)}
    y_at = (y, 1 - y)

    def dev(ss, bb, yy):
        xx = ss * (1 - c) + bb * c
        zz = bb * (1 - c) + ss * c
        return ((zz * 2 + yy) * n + xx) * 2 + c

    sibling = f + 1 - 2 * c
    up, down = dev(s, big_at[1], y), dev(s, big_at[-1], y)
    up_two, down_two = dev(s, big_at[2], y), dev(s, big_at[-2], y)

    def remote(src, dst, sems, target):
        return pltpu.make_async_remote_copy(
            src_ref=src,
            dst_ref=dst,
            send_sem=sems[0],
            recv_sem=sems[1],
            device_id={"fsdp": target},
            device_id_type=MESH,
        )

    loads = [
        pltpu.make_async_copy(src, dst, sem_in.at[i])
        for i, (src, dst) in enumerate(
            [
                (weight_hbm.at[0], weight),
                (gain_hbm, gain),
                (acts_hbm.at[0], acts),
                (targets_hbm.at[0], targets),
                (first_hbm.at[0], first),
                (second_hbm.at[0], second),
                (gain_first_hbm, gain_first),
                (gain_second_hbm, gain_second),
                (base_hbm, base),
            ]
        )
    ]
    loads[0].start()
    loads[1].start()

    peers = [dev(small_at[k], b, y_at[d]) for d, k in PLACES]

    barrier = pltpu.get_barrier_semaphore()
    greeted = [{"rep": lax.rem(rep + k, n_rep)} for k in range(1, n_rep)]
    nearby = peers[:0:-1] + [up_two, down_two, up, down, sibling]
    greeted += [{"fsdp": target} for target in nearby]
    for target in greeted:
        pl.semaphore_signal(barrier, inc=1, device_id=target, device_id_type=MESH)
    for load in loads[2:]:
        load.start()

    loads[0].wait()
    loads[1].wait()
    row_ids = lax.broadcasted_iota(jnp.int32, (rows, rows), 0)
    lane_ids = lax.broadcasted_iota(jnp.int32, (rows, rows), 1)
    eye = row_ids == lane_ids

    def to_column(row):
        return jnp.sum(jnp.where(eye, jnp.broadcast_to(row, (rows, rows)), 0.0), axis=1, keepdims=True)

    def to_row(column):
        return jnp.sum(jnp.where(eye, jnp.broadcast_to(column, (rows, rows)), 0.0), axis=0, keepdims=True)

    gain_used = to_column(gain[...].astype(jnp.bfloat16).astype(jnp.float32))
    low_weight = weight[...].astype(jnp.bfloat16).astype(jnp.float32)
    full_w[c, b, 0] = (gain_used * low_weight).astype(jnp.bfloat16)
    pl.semaphore_wait(barrier, len(greeted))

    gather_peers = [
        remote(
            full_w.at[c, b, 0],
            full_w.at[c, b, MIRROR[p]],
            (sem_send.at[0], sem_peers.at[MIRROR[p] // 4]),
            peers[p],
        )
        for p in range(1, len(PLACES))
    ]
    for copy in reversed(gather_peers):
        copy.start()

    loads[2].wait()
    width = d_model // n

    def prepare(i, total):
        columns = pl.ds(pl.multiple_of(i * width, width), width)
        block = acts[:, columns]
        acts_t[i] = block.T.reshape(2, n, 2, rows, tokens)
        wide = block.astype(jnp.float32)
        square = wide * wide
        for j in range(width // 128):
            total = total + square[:, j * 128 : (j + 1) * 128]
        return total

    squares = lax.fori_loop(0, n, prepare, jnp.zeros((tokens, 128), jnp.float32))
    factor = lax.rsqrt(jnp.sum(squares, axis=1, keepdims=True) / d_model + norm_eps)
    keys_t[...] = jnp.zeros_like(keys_t)
    loads[3].wait()

    def at(j):
        return (pl.ds(j * 4, 4),)

    def part(ref, j):
        return ref.at[at(j)]

    def big(step, slot, src, dst, target, quarters=range(SUBS), each=True):
        return [
            remote(
                part(src, j),
                part(dst, j),
                (sem_send.at[step], sem_big.at[slot + (j if each else 0)]),
                target,
            )
            for j in quarters
        ]

    def landed(dst, sem):
        remote(dst, dst, (sem_send.at[0], sem), sibling).wait_recv()

    def sent(src, step):
        remote(src, src, (sem_send.at[step], sem_big.at[0]), sibling).wait_send()

    def gathered(offset):
        return full_w.at[c, big_at[offset]]

    def gather_core(i, owner, place):
        chunk = full_w.at[owner, place]
        return remote(chunk, chunk, (sem_send.at[2], sem_core.at[0, i]), sibling)

    def chunk_acts(owner, small, place):
        pieces = []
        for d, k in PLACES:
            zz = place * (1 - owner) + small[k] * owner
            xx = small[k] * (1 - owner) + place * owner
            pieces.append(acts_t[zz, y_at[d], xx, owner])
        return jnp.concatenate(pieces, axis=0)

    deep = 2 * n * rows

    def forward(owner, small, place):
        keys_t[...] += lax.dot_general(
            full_w[owner, place].reshape(deep, 128),
            chunk_acts(owner, small, place),
            (((0,), (0,)), ((), ())),
            preferred_element_type=jnp.float32,
        )

    core_offsets = [0, -2, 2, -1, 1, -3, 3, -4]

    def gather_core_last(j, owner, place):
        quarter = part(full_w.at[owner, place], j)
        return remote(quarter, quarter, (sem_send.at[2], sem_core.at[0, n - 1]), sibling)

    def send_core(i):
        gather_core(i, c, big_at[core_offsets[i]]).start()

    def from_sibling(i):
        gather_core(i, 1 - c, small_at[core_offsets[i]]).wait_recv()
        forward(1 - c, big_at, small_at[core_offsets[i]])

    def forward_own(i):
        forward(c, small_at, big_at[core_offsets[i]])

    two_up = big(1, 0, gathered(0), gathered(0), up_two)
    two_down = big(1, 4, gathered(0), gathered(0), down_two)
    one_up = big(1, 8, gathered(0), gathered(0), up, each=False)
    one_down = big(1, 9, gathered(0), gathered(0), down, each=False)
    three_up = big(1, 10, gathered(-2), gathered(-2), up, each=False)
    three_down = big(1, 11, gathered(2), gathered(2), down, each=False)
    four_up = big(1, 12, gathered(-2), gathered(-2), up_two, FAR_UP)
    four_down = big(1, 12, gathered(2), gathered(2), down_two, FAR_DOWN)
    two_up_in = big(1, 0, gathered(-2), gathered(-2), up_two)
    two_down_in = big(1, 4, gathered(2), gathered(2), down_two)
    four_in = big(1, 12, gathered(-4), gathered(-4), up_two)

    for j in range(SUBS):
        first_row = max(4 * j, 1)
        landed(full_w.at[c, b, pl.ds(first_row, 4 * j + 4 - first_row)], sem_peers.at[j])
        two_up[j].start()
        two_down[j].start()
        one_up[j].start()
        one_down[j].start()
    send_core(0)
    forward_own(0)
    for j in range(SUBS):
        two_up_in[j].wait_recv()
        if j in FAR_UP:
            four_up[FAR_UP.index(j)].start()
        three_up[j].start()
        two_down_in[j].wait_recv()
        if j in FAR_DOWN:
            four_down[FAR_DOWN.index(j)].start()
        three_down[j].start()
    send_core(1)
    send_core(2)
    from_sibling(0)
    landed(gathered(-1), sem_big.at[8])
    landed(gathered(1), sem_big.at[9])
    send_core(3)
    send_core(4)
    for i in range(1, 5):
        forward_own(i)
    for i in range(1, 5):
        from_sibling(i)
    landed(gathered(-3), sem_big.at[10])
    landed(gathered(3), sem_big.at[11])
    send_core(5)
    send_core(6)
    forward_own(5)
    forward_own(6)
    for j in range(SUBS):
        four_in[j].wait_recv()
        gather_core_last(j, c, big_at[-4]).start()
    forward_own(7)
    for i in range(5, 8):
        from_sibling(i)

    residual = keys_t[...].T * factor * root_scale - targets[...].astype(jnp.float32)
    scaled = (residual * factor).astype(jnp.bfloat16)

    def backward(owner, small, place):
        block = jnp.dot(chunk_acts(owner, small, place), scaled, preferred_element_type=jnp.float32)
        grads[owner, place] = block.astype(jnp.bfloat16).reshape(2 * n, rows, 128)

    offsets = [4, -3, 3, -1, 1, -2, 2, 0]

    def reduce_core(i, owner, place):
        return remote(
            grads.at[owner, place], from_core.at[place], (sem_send.at[3], sem_core.at[1, i]), sibling
        )

    def own(offset, j):
        chunk = big_at[offset]
        return grads[(c, chunk, *at(j))].astype(jnp.float32) + from_core[
            (chunk, *at(j))
        ].astype(jnp.float32)

    far_down = big(4, 16, out_far, in_far, down_two, FAR_DOWN)
    far_up = big(4, 16, out_far, in_far, up_two, FAR_UP)
    three = [
        big(4, 20, out_three.at[0], in_three.at[0], down),
        big(4, 24, out_three.at[1], in_three.at[1], up),
    ]
    two = [
        big(4, 28, out_two.at[0], in_two.at[0], down_two),
        big(4, 32, out_two.at[1], in_two.at[1], up_two),
    ]
    one = [
        big(4, 36, out_one.at[0], in_one.at[0], down, each=False),
        big(4, 37, out_one.at[1], in_one.at[1], up, each=False),
    ]
    far = {**dict(zip(FAR_DOWN, far_down)), **dict(zip(FAR_UP, far_up))}

    def pass_on(*group):
        for offset in group:
            reduce_core(offsets.index(offset), c, big_at[offset]).wait_recv()
        for j in reversed(range(SUBS)):
            for offset in group:
                side = int(offset > 0)
                value = own(offset, j)
                if abs(offset) == 2:
                    three[side][j].wait_recv()
                    value = value + in_three[(side, *at(j))].astype(jnp.float32)
                    if j in (FAR_DOWN, FAR_UP)[side]:
                        far[j].wait_recv()
                        value = value + in_far[at(j)].astype(jnp.float32)
                low = value.astype(jnp.bfloat16)
                if offset == 4:
                    out_far[at(j)] = low
                    far[j].start()
                else:
                    box, copies = {3: (out_three, three), 2: (out_two, two), 1: (out_one, one)}[abs(offset)]
                    box[(side, *at(j))] = low
                    copies[side][j].start()

    for i, offset in enumerate(offsets):
        backward(1 - c, big_at, small_at[offset])
        reduce_core(i, 1 - c, small_at[offset]).start()
        backward(c, small_at, big_at[offset])
        if 2 <= i < 7:
            pass_on(offsets[i - 2])
    pass_on(-2, 2)
    reduce_core(len(offsets) - 1, c, b).wait_recv()

    reduce_peers = [
        remote(
            mine.at[p],
            from_peers.at[MIRROR[p]],
            (sem_send.at[5], sem_peers.at[SUBS]),
            peers[p],
        )
        for p in range(1, len(PLACES))
    ]
    for side in range(2):
        landed(in_one.at[side], sem_big.at[36 + side])
    for j in reversed(range(SUBS)):
        value = own(0, j)
        for side in range(2):
            value = value + in_one[(side, *at(j))].astype(jnp.float32)
        for side in range(2):
            two[side][j].wait_recv()
            value = value + in_two[(side, *at(j))].astype(jnp.float32)
        mine[at(j)] = value.astype(jnp.bfloat16)
        for p in reversed(range(max(4 * j, 1), 4 * j + 4)):
            reduce_peers[p - 1].start()
    for load in loads[4:]:
        load.wait()
    grad_sum = mine[0].astype(jnp.float32)
    others = pl.ds(1, len(PLACES) - 1)
    landed(from_peers.at[others], sem_peers.at[SUBS])
    for p in range(1, len(PLACES)):
        grad_sum = grad_sum + from_peers[p].astype(jnp.float32)

    grad_weight = gain_used * grad_sum * root_scale / token_count
    inner_weight = adam_step(weight[...], grad_weight, first[...], second[...])
    drifts[rep] = base[...] - inner_weight
    rep_copies = []
    for k in range(1, n_rep):
        rep_copies.append(
            pltpu.make_async_remote_copy(
                src_ref=drifts.at[rep],
                dst_ref=drifts.at[rep],
                send_sem=sem_rep.at[0, k - 1],
                recv_sem=sem_rep.at[1, k - 1],
                device_id={"rep": lax.rem(rep + k, n_rep)},
                device_id_type=MESH,
            )
        )
        rep_copies[-1].start()

    gain_sum = to_row(jnp.sum(grad_sum * low_weight, axis=1, keepdims=True) * root_scale)
    new_gain_ref[...] = adam_step(gain[...], gain_sum / token_count, gain_first[...], gain_second[...])

    sent(full_w.at[c, b, others], 0)
    sent(full_w.at[c, pl.ds(0, 7)], 1)
    sent(full_w.at[c], 2)
    sent(from_core, 3)
    sent(from_core.at[pl.ds(0, 7)], 4)
    sent(mine.at[others], 5)
    for copy in rep_copies:
        copy.wait_recv()
    average = drifts[0]
    for k in range(1, n_rep):
        average = average + drifts[k]
    average_ref[...] = average / n_rep
    inner_ref[...] = inner_weight

    for copy in rep_copies:
        copy.wait_send()


def per_device(*args):
    acts, targets, weight, _, _, gain = args[:6]
    n_rep = lax.axis_size("rep")
    n = math.isqrt(lax.axis_size("fsdp") // 4)
    tokens, d_model = acts.shape[1:]
    rows, head = weight.shape[1:]
    low, wide = jnp.bfloat16, jnp.float32
    chunk = (2 * n, rows, head)
    dma = pltpu.SemaphoreType.DMA
    scratch = [
        pltpu.VMEM((tokens, d_model), low),
        pltpu.VMEM((n, 2, n, 2, rows, tokens), low),
        pltpu.VMEM((tokens, head), low),
        pltpu.VMEM((rows, head), wide),
        pltpu.VMEM((rows, head), wide),
        pltpu.VMEM((rows, head), wide),
        pltpu.VMEM((1, rows), wide),
        pltpu.VMEM((1, rows), wide),
        pltpu.VMEM((1, rows), wide),
        pltpu.VMEM((rows, head), wide),
        pltpu.VMEM((2, n, *chunk), low),
        pltpu.VMEM((2, n, *chunk), low),
        pltpu.VMEM((head, tokens), wide),
        pltpu.VMEM((n, *chunk), low),
        pltpu.VMEM(chunk, low),
        pltpu.VMEM((2, *chunk), low),
        pltpu.VMEM((2, *chunk), low),
        pltpu.VMEM((2, *chunk), low),
        pltpu.VMEM(chunk, low),
        pltpu.VMEM((2, *chunk), low),
        pltpu.VMEM((2, *chunk), low),
        pltpu.VMEM((2, *chunk), low),
        pltpu.VMEM(chunk, low),
        pltpu.VMEM((2 * n, rows, head), low),
        pltpu.VMEM((n_rep, rows, head), wide),
        dma((9,)),
        dma((6,)),
        dma((SUBS + 1,)),
        dma((38,)),
        dma((2, n)),
        dma((2, max(n_rep - 1, 1))),
    ]
    inner_weight, new_gain, average = pl.pallas_call(
        functools.partial(kernel, n, n_rep),
        out_shape=(
            pltpu.VMEM((rows, head), wide),
            pltpu.VMEM((1, rows), wide),
            pltpu.VMEM((rows, head), wide),
        ),
        in_specs=[pl.BlockSpec(memory_space=pltpu.HBM)] * 9,
        out_specs=tuple([pl.BlockSpec(memory_space=pltpu.VMEM)] * 3),
        scratch_shapes=scratch,
        compiler_params=pltpu.CompilerParams(
            collective_id=0, has_side_effects=True, vmem_limit_bytes=48 * 1024 * 1024
        ),
        cost_estimate=pl.CostEstimate(
            flops=4 * tokens * d_model * head, bytes_accessed=2 * tokens * d_model, transcendentals=0
        ),
    )(*[pltpu.with_memory_space_constraint(arg, pltpu.HBM) for arg in args[:-1]])
    base, momentum = args[-2:]
    new_momentum = nesterov * momentum + average
    new_base = base - outer_rate * (average + nesterov * new_momentum)
    new_weight = mixing * inner_weight + (1.0 - mixing) * new_base
    return new_weight[None], new_gain, new_base, new_momentum


def solution(mesh):
    return jax.shard_map(
        per_device,
        mesh=mesh,
        in_specs=(
            P("rep", "fsdp", None),
            P("rep", "fsdp", None),
            P("rep", "fsdp", None),
            P("rep", "fsdp", None),
            P("rep", "fsdp", None),
            P("rep", "fsdp"),
            P("rep", "fsdp"),
            P("rep", "fsdp"),
            P("fsdp", None),
            P("fsdp", None),
        ),
        out_specs=(P("rep", "fsdp", None), P("rep", "fsdp"), P("fsdp", None), P("fsdp", None)),
        check_vma=False,
    )
```

```python
import functools
import math

import jax
import jax.numpy as jnp
from jax import lax
from jax.experimental import pallas as pl
from jax.experimental.pallas import tpu as pltpu
from jax.sharding import PartitionSpec as P

MESH = pl.DeviceIdType.MESH

norm_eps = 1e-05
adam_eps = 1e-08
beta_first = 0.9
beta_second = 0.95
bias_first = 1.0 - 0.9**50
bias_second = 1.0 - 0.95**50
inner_rate = 0.1
decay_rate = 0.1
outer_rate = 0.7
nesterov = 0.9
mixing = 0.5

SUBS = 4
PLACES = [(0, 0), (0, 1), (0, -1), (1, 0), (1, 1), (1, -1), (0, 2), (0, -2)]
PLACES += [(1, 2), (1, -2), (0, 3), (0, -3), (1, 3), (1, -3), (0, 4), (1, 4)]
MIRROR = [PLACES.index((d, k if k == 4 else -k)) for d, k in PLACES]
FAR_UP, FAR_DOWN = (0, 2), (1, 3)


def adam_step(param, grad, first, second):
    first = beta_first * first + (1.0 - beta_first) * grad
    second = beta_second * second + (1.0 - beta_second) * grad * grad
    update = first / bias_first / (jnp.sqrt(second / bias_second) + adam_eps)
    return param - inner_rate * (update + decay_rate * param)


def kernel(
    n,
    n_rep,
    acts_hbm,
    targets_hbm,
    weight_hbm,
    first_hbm,
    second_hbm,
    gain_hbm,
    gain_first_hbm,
    gain_second_hbm,
    base_hbm,
    inner_ref,
    new_gain_ref,
    average_ref,
    acts,
    acts_t,
    targets,
    weight,
    first,
    second,
    gain,
    gain_first,
    gain_second,
    base,
    full_w,
    grads,
    keys_t,
    from_core,
    out_far,
    out_three,
    out_two,
    out_one,
    in_far,
    in_three,
    in_two,
    in_one,
    mine,
    from_peers,
    drifts,
    sem_in,
    sem_send,
    sem_peers,
    sem_big,
    sem_core,
    sem_rep,
):
    tokens, d_model = acts.shape
    rows = weight.shape[0]
    token_count = tokens * 4 * n * n
    root_scale = 1.0 / math.sqrt(d_model)

    rep = lax.axis_index("rep")
    f = lax.axis_index("fsdp")
    c = lax.rem(f, 2)
    x = lax.rem(lax.div(f, 2), n)
    y = lax.rem(lax.div(f, 2 * n), 2)
    z = lax.div(f, 4 * n)
    s = x * (1 - c) + z * c
    b = z * (1 - c) + x * c

    small_at = {k: lax.rem(s + n + k, n) for k in range(-4, 5)}
    big_at = {k: lax.rem(b + n + k, n) for k in range(-4, 5)}
    y_at = (y, 1 - y)

    def dev(ss, bb, yy):
        xx = ss * (1 - c) + bb * c
        zz = bb * (1 - c) + ss * c
        return ((zz * 2 + yy) * n + xx) * 2 + c

    sibling = f + 1 - 2 * c
    up, down = dev(s, big_at[1], y), dev(s, big_at[-1], y)
    up_two, down_two = dev(s, big_at[2], y), dev(s, big_at[-2], y)

    def remote(src, dst, sems, target):
        return pltpu.make_async_remote_copy(
            src_ref=src,
            dst_ref=dst,
            send_sem=sems[0],
            recv_sem=sems[1],
            device_id={"fsdp": target},
            device_id_type=MESH,
        )

    loads = [
        pltpu.make_async_copy(src, dst, sem_in.at[i])
        for i, (src, dst) in enumerate(
            [
                (weight_hbm.at[0], weight),
                (gain_hbm, gain),
                (acts_hbm.at[0], acts),
                (targets_hbm.at[0], targets),
                (first_hbm.at[0], first),
                (second_hbm.at[0], second),
                (gain_first_hbm, gain_first),
                (gain_second_hbm, gain_second),
                (base_hbm, base),
            ]
        )
    ]
    loads[0].start()
    loads[1].start()

    peers = [dev(small_at[k], b, y_at[d]) for d, k in PLACES]

    barrier = pltpu.get_barrier_semaphore()
    greeted = [{"rep": lax.rem(rep + k, n_rep)} for k in range(1, n_rep)]
    nearby = peers[:0:-1] + [up_two, down_two, up, down, sibling]
    greeted += [{"fsdp": target} for target in nearby]
    for target in greeted:
        pl.semaphore_signal(barrier, inc=1, device_id=target, device_id_type=MESH)
    for load in loads[2:]:
        load.start()

    loads[0].wait()
    loads[1].wait()
    row_ids = lax.broadcasted_iota(jnp.int32, (rows, rows), 0)
    lane_ids = lax.broadcasted_iota(jnp.int32, (rows, rows), 1)
    eye = row_ids == lane_ids

    def to_column(row):
        return jnp.sum(jnp.where(eye, jnp.broadcast_to(row, (rows, rows)), 0.0), axis=1, keepdims=True)

    def to_row(column):
        return jnp.sum(jnp.where(eye, jnp.broadcast_to(column, (rows, rows)), 0.0), axis=0, keepdims=True)

    gain_used = to_column(gain[...].astype(jnp.bfloat16).astype(jnp.float32))
    low_weight = weight[...].astype(jnp.bfloat16).astype(jnp.float32)
    full_w[c, b, 0] = (gain_used * low_weight).astype(jnp.bfloat16)
    pl.semaphore_wait(barrier, len(greeted))

    gather_peers = [
        remote(
            full_w.at[c, b, 0],
            full_w.at[c, b, MIRROR[p]],
            (sem_send.at[0], sem_peers.at[MIRROR[p] // 4]),
            peers[p],
        )
        for p in range(1, len(PLACES))
    ]
    for copy in reversed(gather_peers):
        copy.start()

    loads[2].wait()
    width = d_model // n

    def prepare(i, total):
        columns = pl.ds(pl.multiple_of(i * width, width), width)
        block = acts[:, columns]
        acts_t[i] = block.T.reshape(2, n, 2, rows, tokens)
        wide = block.astype(jnp.float32)
        square = wide * wide
        for j in range(width // 128):
            total = total + square[:, j * 128 : (j + 1) * 128]
        return total

    squares = lax.fori_loop(0, n, prepare, jnp.zeros((tokens, 128), jnp.float32))
    factor = lax.rsqrt(jnp.sum(squares, axis=1, keepdims=True) / d_model + norm_eps)
    keys_t[...] = jnp.zeros_like(keys_t)
    loads[3].wait()

    def at(j):
        return (pl.ds(j * 4, 4),)

    def part(ref, j):
        return ref.at[at(j)]

    def big(step, slot, src, dst, target, quarters=range(SUBS), each=True):
        return [
            remote(
                part(src, j),
                part(dst, j),
                (sem_send.at[step], sem_big.at[slot + (j if each else 0)]),
                target,
            )
            for j in quarters
        ]

    def landed(dst, sem):
        remote(dst, dst, (sem_send.at[0], sem), sibling).wait_recv()

    def sent(src, step):
        remote(src, src, (sem_send.at[step], sem_big.at[0]), sibling).wait_send()

    def gathered(offset):
        return full_w.at[c, big_at[offset]]

    def gather_core(i, owner, place):
        chunk = full_w.at[owner, place]
        return remote(chunk, chunk, (sem_send.at[2], sem_core.at[0, i]), sibling)

    def chunk_acts(owner, small, place):
        pieces = []
        for d, k in PLACES:
            zz = place * (1 - owner) + small[k] * owner
            xx = small[k] * (1 - owner) + place * owner
            pieces.append(acts_t[zz, y_at[d], xx, owner])
        return jnp.concatenate(pieces, axis=0)

    deep = 2 * n * rows

    def forward(owner, small, place):
        keys_t[...] += lax.dot_general(
            full_w[owner, place].reshape(deep, 128),
            chunk_acts(owner, small, place),
            (((0,), (0,)), ((), ())),
            preferred_element_type=jnp.float32,
        )

    core_offsets = [0, -2, 2, -1, 1, -3, 3, -4]

    def gather_core_last(j, owner, place):
        quarter = part(full_w.at[owner, place], j)
        return remote(quarter, quarter, (sem_send.at[2], sem_core.at[0, n - 1]), sibling)

    def send_core(i):
        gather_core(i, c, big_at[core_offsets[i]]).start()

    def from_sibling(i):
        gather_core(i, 1 - c, small_at[core_offsets[i]]).wait_recv()
        forward(1 - c, big_at, small_at[core_offsets[i]])

    def forward_own(i):
        forward(c, small_at, big_at[core_offsets[i]])

    two_up = big(1, 0, gathered(0), gathered(0), up_two)
    two_down = big(1, 4, gathered(0), gathered(0), down_two)
    one_up = big(1, 8, gathered(0), gathered(0), up, each=False)
    one_down = big(1, 9, gathered(0), gathered(0), down, each=False)
    three_up = big(1, 10, gathered(-2), gathered(-2), up, each=False)
    three_down = big(1, 11, gathered(2), gathered(2), down, each=False)
    four_up = big(1, 12, gathered(-2), gathered(-2), up_two, FAR_UP)
    four_down = big(1, 12, gathered(2), gathered(2), down_two, FAR_DOWN)
    two_up_in = big(1, 0, gathered(-2), gathered(-2), up_two)
    two_down_in = big(1, 4, gathered(2), gathered(2), down_two)
    four_in = big(1, 12, gathered(-4), gathered(-4), up_two)

    for j in range(SUBS):
        first_row = max(4 * j, 1)
        landed(full_w.at[c, b, pl.ds(first_row, 4 * j + 4 - first_row)], sem_peers.at[j])
        two_up[j].start()
        two_down[j].start()
        one_up[j].start()
        one_down[j].start()
    send_core(0)
    forward_own(0)
    for j in range(SUBS):
        two_up_in[j].wait_recv()
        if j in FAR_UP:
            four_up[FAR_UP.index(j)].start()
        three_up[j].start()
        two_down_in[j].wait_recv()
        if j in FAR_DOWN:
            four_down[FAR_DOWN.index(j)].start()
        three_down[j].start()
    send_core(1)
    send_core(2)
    from_sibling(0)
    landed(gathered(-1), sem_big.at[8])
    landed(gathered(1), sem_big.at[9])
    send_core(3)
    send_core(4)
    for i in range(1, 5):
        forward_own(i)
    for i in range(1, 5):
        from_sibling(i)
    landed(gathered(-3), sem_big.at[10])
    landed(gathered(3), sem_big.at[11])
    send_core(5)
    send_core(6)
    forward_own(5)
    forward_own(6)
    for j in range(SUBS):
        four_in[j].wait_recv()
        gather_core_last(j, c, big_at[-4]).start()
    forward_own(7)
    for i in range(5, 8):
        from_sibling(i)

    residual = keys_t[...].T * factor * root_scale - targets[...].astype(jnp.float32)
    scaled = (residual * factor).astype(jnp.bfloat16)

    def backward(owner, small, place):
        block = jnp.dot(chunk_acts(owner, small, place), scaled, preferred_element_type=jnp.float32)
        grads[owner, place] = block.astype(jnp.bfloat16).reshape(2 * n, rows, 128)

    offsets = [4, -3, 3, -1, 1, -2, 2, 0]

    def reduce_core(i, owner, place):
        return remote(
            grads.at[owner, place], from_core.at[place], (sem_send.at[3], sem_core.at[1, i]), sibling
        )

    def own(offset, j):
        chunk = big_at[offset]
        return grads[(c, chunk, *at(j))].astype(jnp.float32) + from_core[
            (chunk, *at(j))
        ].astype(jnp.float32)

    far_down = big(4, 16, out_far, in_far, down_two, FAR_DOWN)
    far_up = big(4, 16, out_far, in_far, up_two, FAR_UP)
    three = [
        big(4, 20, out_three.at[0], in_three.at[0], down),
        big(4, 24, out_three.at[1], in_three.at[1], up),
    ]
    two = [
        big(4, 28, out_two.at[0], in_two.at[0], down_two),
        big(4, 32, out_two.at[1], in_two.at[1], up_two),
    ]
    one = [
        big(4, 36, out_one.at[0], in_one.at[0], down, each=False),
        big(4, 37, out_one.at[1], in_one.at[1], up, each=False),
    ]
    far = {**dict(zip(FAR_DOWN, far_down)), **dict(zip(FAR_UP, far_up))}

    def pass_on(*group):
        for offset in group:
            reduce_core(offsets.index(offset), c, big_at[offset]).wait_recv()
        for j in reversed(range(SUBS)):
            for offset in group:
                side = int(offset > 0)
                value = own(offset, j)
                if abs(offset) == 2:
                    three[side][j].wait_recv()
                    value = value + in_three[(side, *at(j))].astype(jnp.float32)
                    if j in (FAR_DOWN, FAR_UP)[side]:
                        far[j].wait_recv()
                        value = value + in_far[at(j)].astype(jnp.float32)
                low = value.astype(jnp.bfloat16)
                if offset == 4:
                    out_far[at(j)] = low
                    far[j].start()
                else:
                    box, copies = {3: (out_three, three), 2: (out_two, two), 1: (out_one, one)}[abs(offset)]
                    box[(side, *at(j))] = low
                    copies[side][j].start()

    def produce(owner, *steps):
        for i in steps:
            offset = offsets[i]
            x_at = {k: small_at[k] * (1 - c) + big_at[k] * c for k in small_at}
            z_at = {k: big_at[k] * (1 - c) + small_at[k] * c for k in small_at}
            if owner == 0:
                backward(0, x_at, z_at[offset])
            else:
                backward(1, z_at, x_at[offset])

            @pl.when(c == 1 - owner)
            def _():
                reduce_core(i, 1 - c, small_at[offset]).start()

    produce(0, 0, 1, 2)
    produce(1, 0, 1, 2)
    pass_on(4)
    pass_on(-3)
    pass_on(3)
    produce(0, 3, 4)
    produce(1, 3, 4)
    pass_on(-1)
    produce(0, 5, 6)
    produce(1, 5, 6)
    pass_on(1)
    produce(0, 7)
    produce(1, 7)
    pass_on(-2, 2)
    reduce_core(len(offsets) - 1, c, b).wait_recv()

    reduce_peers = [
        remote(
            mine.at[p],
            from_peers.at[MIRROR[p]],
            (sem_send.at[5], sem_peers.at[SUBS]),
            peers[p],
        )
        for p in range(1, len(PLACES))
    ]
    for side in range(2):
        landed(in_one.at[side], sem_big.at[36 + side])
    for j in reversed(range(SUBS)):
        value = own(0, j)
        for side in range(2):
            value = value + in_one[(side, *at(j))].astype(jnp.float32)
        for side in range(2):
            two[side][j].wait_recv()
            value = value + in_two[(side, *at(j))].astype(jnp.float32)
        mine[at(j)] = value.astype(jnp.bfloat16)
        for p in reversed(range(max(4 * j, 1), 4 * j + 4)):
            reduce_peers[p - 1].start()
    for load in loads[4:]:
        load.wait()
    grad_sum = mine[0].astype(jnp.float32)
    others = pl.ds(1, len(PLACES) - 1)
    landed(from_peers.at[others], sem_peers.at[SUBS])
    for p in range(1, len(PLACES)):
        grad_sum = grad_sum + from_peers[p].astype(jnp.float32)

    grad_weight = gain_used * grad_sum * root_scale / token_count
    inner_weight = adam_step(weight[...], grad_weight, first[...], second[...])
    drifts[rep] = base[...] - inner_weight
    rep_copies = []
    for k in range(1, n_rep):
        rep_copies.append(
            pltpu.make_async_remote_copy(
                src_ref=drifts.at[rep],
                dst_ref=drifts.at[rep],
                send_sem=sem_rep.at[0, k - 1],
                recv_sem=sem_rep.at[1, k - 1],
                device_id={"rep": lax.rem(rep + k, n_rep)},
                device_id_type=MESH,
            )
        )
        rep_copies[-1].start()

    gain_sum = to_row(jnp.sum(grad_sum * low_weight, axis=1, keepdims=True) * root_scale)
    new_gain_ref[...] = adam_step(gain[...], gain_sum / token_count, gain_first[...], gain_second[...])

    sent(full_w.at[c, b, others], 0)
    sent(full_w.at[c, pl.ds(0, 7)], 1)
    sent(full_w.at[c], 2)
    sent(from_core, 3)
    sent(from_core.at[pl.ds(0, 7)], 4)
    sent(mine.at[others], 5)
    for copy in rep_copies:
        copy.wait_recv()
    average = drifts[0]
    for k in range(1, n_rep):
        average = average + drifts[k]
    average_ref[...] = average / n_rep
    inner_ref[...] = inner_weight

    for copy in rep_copies:
        copy.wait_send()


def per_device(*args):
    acts, targets, weight, _, _, gain = args[:6]
    n_rep = lax.axis_size("rep")
    n = math.isqrt(lax.axis_size("fsdp") // 4)
    tokens, d_model = acts.shape[1:]
    rows, head = weight.shape[1:]
    low, wide = jnp.bfloat16, jnp.float32
    chunk = (2 * n, rows, head)
    dma = pltpu.SemaphoreType.DMA
    scratch = [
        pltpu.VMEM((tokens, d_model), low),
        pltpu.VMEM((n, 2, n, 2, rows, tokens), low),
        pltpu.VMEM((tokens, head), low),
        pltpu.VMEM((rows, head), wide),
        pltpu.VMEM((rows, head), wide),
        pltpu.VMEM((rows, head), wide),
        pltpu.VMEM((1, rows), wide),
        pltpu.VMEM((1, rows), wide),
        pltpu.VMEM((1, rows), wide),
        pltpu.VMEM((rows, head), wide),
        pltpu.VMEM((2, n, *chunk), low),
        pltpu.VMEM((2, n, *chunk), low),
        pltpu.VMEM((head, tokens), wide),
        pltpu.VMEM((n, *chunk), low),
        pltpu.VMEM(chunk, low),
        pltpu.VMEM((2, *chunk), low),
        pltpu.VMEM((2, *chunk), low),
        pltpu.VMEM((2, *chunk), low),
        pltpu.VMEM(chunk, low),
        pltpu.VMEM((2, *chunk), low),
        pltpu.VMEM((2, *chunk), low),
        pltpu.VMEM((2, *chunk), low),
        pltpu.VMEM(chunk, low),
        pltpu.VMEM((2 * n, rows, head), low),
        pltpu.VMEM((n_rep, rows, head), wide),
        dma((9,)),
        dma((6,)),
        dma((SUBS + 1,)),
        dma((38,)),
        dma((2, n)),
        dma((2, max(n_rep - 1, 1))),
    ]
    inner_weight, new_gain, average = pl.pallas_call(
        functools.partial(kernel, n, n_rep),
        out_shape=(
            pltpu.VMEM((rows, head), wide),
            pltpu.VMEM((1, rows), wide),
            pltpu.VMEM((rows, head), wide),
        ),
        in_specs=[pl.BlockSpec(memory_space=pltpu.HBM)] * 9,
        out_specs=tuple([pl.BlockSpec(memory_space=pltpu.VMEM)] * 3),
        scratch_shapes=scratch,
        compiler_params=pltpu.CompilerParams(
            collective_id=0, has_side_effects=True, vmem_limit_bytes=48 * 1024 * 1024
        ),
        cost_estimate=pl.CostEstimate(
            flops=4 * tokens * d_model * head, bytes_accessed=2 * tokens * d_model, transcendentals=0
        ),
    )(*[pltpu.with_memory_space_constraint(arg, pltpu.HBM) for arg in args[:-1]])
    base, momentum = args[-2:]
    new_momentum = nesterov * momentum + average
    new_base = base - outer_rate * (average + nesterov * new_momentum)
    new_weight = mixing * inner_weight + (1.0 - mixing) * new_base
    return new_weight[None], new_gain, new_base, new_momentum


def solution(mesh):
    return jax.shard_map(
        per_device,
        mesh=mesh,
        in_specs=(
            P("rep", "fsdp", None),
            P("rep", "fsdp", None),
            P("rep", "fsdp", None),
            P("rep", "fsdp", None),
            P("rep", "fsdp", None),
            P("rep", "fsdp"),
            P("rep", "fsdp"),
            P("rep", "fsdp"),
            P("fsdp", None),
            P("fsdp", None),
        ),
        out_specs=(P("rep", "fsdp", None), P("rep", "fsdp"), P("fsdp", None), P("fsdp", None)),
        check_vma=False,
    )
```
